32 devices in a mesh: seq: 16 (over z, y, x), mlp: 2 (over core).
Axes of the slice: x: 2, y: 2, z: 4, core: 2. Of those that a mesh axis runs over, the one named last changes fastest.
Arguments:
- queries: bfloat16 [4096, 3072], P('seq', 'mlp'), may hold values from -5 to 5
- key_vectors: bfloat16 [4096, 3072], P('seq', 'mlp'), may hold values from -5 to 5
- value_vectors: bfloat16 [4096, 3072], P('seq', 'mlp'), may hold values from -6 to 6
- head_kinds: int32 [24], P('mlp'), may hold values from 0 to 1
- block_masks: int32 [24, 2, 2], P('mlp'), may hold values from 0 to 1, as said below
- order_map: int32 [256], replicated, may hold values from 0 to 255, as said below
- out_weight: bfloat16 [3072, 3072], P('seq', 'mlp'), may hold values from -0.109375 to 0.109375
- gate_values: float32 [3072], P('mlp'), may hold values from 0.5 to 2
Outputs:
- gated_output: bfloat16 [4096, 3072], P('seq', 'mlp')
The draws below stay inside these ranges and needn't reach their ends.
Inputs may be any that keep to these rules, and one draw needn't show every extreme that they name: block_masks[h, b, b] = 1 for every head h and block b. A permutation of the 256 positions in which order_map[2 i] is even and order_map[2 i + 1] = order_map[2 i] + 1.
All inputs are finite; a program needn't handle non-finite values.
Results may differ from the reference program's by a relative error of at most 0.0056.
Values may be sent and summed in bfloat16 or wider, within the bound.
A program may use at most 64 MiB of HBM per device.

```python
import math
import jax
import jax.numpy as jnp
from jax import lax

D = 3072
HEADS = 24
HD = 128
BLOCK = 128
POS = 256
FRAMES = 16
TOKENS = 4096
BLOCKS = 2
GROUP = 16


def draw_queries(key, part):
    key = jax.random.fold_in(key, 5)
    first_key = jax.random.fold_in(key, 0)
    values_base = jax.random.normal(first_key, (TOKENS, HEADS * HD), jnp.float32) * 0.35
    return jnp.clip(values_base, -5.0, 5.0).astype(jnp.bfloat16)


def draw_key_vectors(key, part):
    key = jax.random.fold_in(key, 7)
    first_key = jax.random.fold_in(key, 0)
    values_base = jax.random.normal(first_key, (TOKENS, HEADS * HD), jnp.float32) * 0.35
    return jnp.clip(values_base, -5.0, 5.0).astype(jnp.bfloat16)


def draw_block_masks(key, part):
    key = jax.random.fold_in(key, 11)
    first_key, second_key = jax.random.split(key)
    density = jax.random.randint(first_key, (HEADS, 1, 1), 2, 10)
    rolled = jax.random.randint(second_key, (HEADS, BLOCKS, BLOCKS), 0, 10)
    diagonal = jnp.eye(BLOCKS, dtype=jnp.int32)[None, :, :]
    return jnp.maximum((rolled < density).astype(jnp.int32), diagonal)


def draw_order_map(key, part):
    key = jax.random.fold_in(key, 13)
    pair_order = jax.random.permutation(key, POS // 2).astype(jnp.int32)
    return jnp.stack([2 * pair_order, 2 * pair_order + 1], axis=1).reshape(POS).astype(jnp.int32)


def with_ends(values, rng, low, top_value):
    shape = values.shape
    place = [jax.random.randint(jax.random.fold_in(rng, axis), (), 0, shape[axis]) for axis in range(len(shape))]
    values = values.at[tuple(place)].set(low)
    longest = shape.index(max(shape))
    place[longest] = (place[longest] + 1) % shape[longest]
    return values.at[tuple(place)].set(top_value)


def block_levels(key, shape, pieces, smallest, top_value):
    level = 1.0
    for dim, shards_of in pieces:
        heights = jax.random.uniform(jax.random.fold_in(jax.random.fold_in(key, 6), dim), (shards_of,), jnp.float32, smallest / len(pieces), top_value / len(pieces))
        level = level * jnp.repeat(jnp.exp(heights), shape[dim] // shards_of).reshape((-1,) + (1,) * (len(shape) - 1 - dim))
    return level


def scatter_about(own_key, shape, scale, bound, cuts=(), held_as=jnp.bfloat16):
    values = jax.random.normal(own_key, shape, jnp.float32) * scale
    if len(cuts) > 0:
        values = block_levels(own_key, shape, cuts, -0.22, 0.18) * values
    return jnp.clip(values, min=-bound, max=bound).astype(held_as)


def setup_inputs(seed: int = 0) -> dict:
    seeds = jax.random.split(jax.random.key(seed), 9)
    queries = draw_queries(jax.random.fold_in(seeds[8], 71), 0)
    key_vectors = draw_key_vectors(jax.random.fold_in(seeds[8], 71), 0)
    value_vectors = scatter_about(seeds[2], (TOKENS, HEADS * HD), 1.0, 6.0, ((0, 16), (1, 2)))
    head_kinds = with_ends(jax.random.randint(seeds[3], (HEADS,), 0, 2), jax.random.fold_in(seeds[3], 1), 0, 1).astype(jnp.int32)
    block_masks = draw_block_masks(jax.random.fold_in(seeds[8], 71), 0)
    order_map = draw_order_map(jax.random.fold_in(seeds[8], 71), 0)
    out_weight = scatter_about(seeds[6], (HEADS * HD, D), (HEADS * HD) ** -0.5, 0.109375, ((0, 16), (1, 2)))
    gate_values = jnp.clip(0.5 + 1.5 * jax.random.uniform(seeds[7], (D,), jnp.float32) ** block_levels(seeds[7], (D,), ((0, 2),), -0.2, 0.2), 0.5, 2.0)
    return {"queries": queries, "key_vectors": key_vectors, "value_vectors": value_vectors, "head_kinds": head_kinds, "block_masks": block_masks, "order_map": order_map, "out_weight": out_weight, "gate_values": gate_values}


def attend_group(query_rows, key_rows, value_rows, visible):
    score_scale = 1.0 / math.sqrt(HD)
    scores = jnp.dot(query_rows.astype(jnp.float32), key_rows.astype(jnp.float32).T, precision=lax.Precision.HIGHEST) * score_scale
    masked = jnp.where(visible, scores, -jnp.inf)
    row_max = lax.optimization_barrier(jnp.max(masked, axis=1, keepdims=True))
    weights = jnp.where(visible, jnp.exp(scores - row_max), 0.0)
    row_total = lax.optimization_barrier(jnp.sum(weights, axis=1, keepdims=True))
    rounded = lax.optimization_barrier(weights.astype(jnp.bfloat16))
    combined = jnp.dot(rounded.astype(jnp.float32), value_rows.astype(jnp.float32), precision=lax.Precision.HIGHEST)
    return (combined / row_total).astype(jnp.bfloat16)

def reference(queries, key_vectors, value_vectors, head_kinds, block_masks, order_map, out_weight, gate_values):
    spatial = jnp.arange(TOKENS, dtype=jnp.int32)
    slot_table = order_map.reshape(FRAMES, GROUP).astype(jnp.int32)
    frame_starts = jnp.arange(FRAMES, dtype=jnp.int32) * POS
    temporal = (frame_starts[None, None, :] + slot_table[:, :, None]).reshape(TOKENS).astype(jnp.int32)

    def one_head(head_index):
        layout = jnp.where(head_kinds[head_index] == 1, temporal, spatial)
        column_start = (head_index * HD).astype(jnp.int32)
        query_rows = lax.dynamic_slice_in_dim(queries, column_start, HD, 1)[layout].reshape(FRAMES, POS, HD)
        key_rows = lax.dynamic_slice_in_dim(key_vectors, column_start, HD, 1)[layout].reshape(FRAMES, POS, HD)
        value_rows = lax.dynamic_slice_in_dim(value_vectors, column_start, HD, 1)[layout].reshape(FRAMES, POS, HD)
        head_mask = block_masks[head_index] == 1
        visible = jnp.repeat(jnp.repeat(head_mask, BLOCK, axis=0), BLOCK, axis=1)

        def one_group(triple):
            return attend_group(triple[0], triple[1], triple[2], visible)
        results = lax.map(one_group, (query_rows, key_rows, value_rows))
        return jnp.zeros((TOKENS, HD), jnp.bfloat16).at[layout].set(results.reshape(TOKENS, HD))
    per_head = lax.map(one_head, jnp.arange(HEADS, dtype=jnp.int32))
    attended = jnp.transpose(per_head, (1, 0, 2)).reshape(TOKENS, HEADS * HD)
    projected = jnp.dot(attended, out_weight, preferred_element_type=jnp.float32)
    return (gate_values[None, :] * projected).astype(jnp.bfloat16)
```

```python
import functools
import math

import jax
import jax.numpy as jnp
from jax import lax
from jax.experimental import pallas as pl
from jax.experimental.pallas import tpu as pltpu
from jax.sharding import PartitionSpec as P


def attend_rows(query_rows, key_rows, value_rows, visible):
    row_count, head_count, head_depth = query_rows.shape
    score_scale = 1.0 / math.sqrt(head_depth)
    scores = (
        jnp.einsum("qhd,khd->hqk", query_rows, key_rows, preferred_element_type=jnp.float32)
        * score_scale
    )
    row_max = jnp.max(jnp.where(visible, scores, -jnp.inf), axis=2, keepdims=True)
    weights = jnp.where(visible, jnp.exp(scores - row_max), 0.0)
    row_total = jnp.sum(weights, axis=2)
    combined = jnp.einsum(
        "hqk,khd->qhd", weights.astype(jnp.bfloat16), value_rows, preferred_element_type=jnp.float32
    )
    outputs = (combined / jnp.transpose(row_total)[:, :, None]).astype(jnp.bfloat16)
    return outputs


def to_positions(query_rows, key_rows, value_rows, frames, group_size):
    row_width = query_rows.shape[1]
    exchanged = (
        lax.all_to_all(
            query_rows.reshape(frames, group_size, 1, row_width),
            "seq",
            split_axis=0,
            concat_axis=2,
            tiled=True,
        ),
        lax.all_to_all(
            key_rows.reshape(frames, group_size, 1, row_width),
            "seq",
            split_axis=0,
            concat_axis=2,
            tiled=True,
        ),
        lax.all_to_all(
            value_rows.reshape(frames, group_size, 1, row_width),
            "seq",
            split_axis=0,
            concat_axis=2,
            tiled=True,
        ),
    )
    return tuple((member.reshape(group_size * frames, row_width) for member in exchanged))


def to_frames(results, frames, group_size):
    row_width = results.shape[1]
    exchanged = lax.all_to_all(
        results.reshape(1, group_size, frames, row_width),
        "seq",
        split_axis=2,
        concat_axis=0,
        tiled=True,
    )
    return exchanged.reshape(frames * group_size, row_width)


def split_heads(array, head_count):
    return array.reshape(array.shape[0], head_count, array.shape[1] // head_count)


def local(
    queries, key_vectors, value_vectors, head_kinds, block_masks, order_map, out_weight, gate_values
):
    row_count, row_width = queries.shape
    head_count = head_kinds.shape[0]
    frames = lax.axis_size("seq")
    group_size = row_count // frames
    block_size = row_count // block_masks.shape[1]
    inverse = (
        jnp.zeros((row_count,), jnp.int32).at[order_map].set(jnp.arange(row_count, dtype=jnp.int32))
    )
    visible = jnp.repeat(jnp.repeat(block_masks == 1, block_size, axis=1), block_size, axis=2)
    temporal = (head_kinds == 1)[None, :, None]
    moved_queries, moved_keys, moved_values = to_positions(
        queries[order_map], key_vectors[order_map], value_vectors[order_map], frames, group_size
    )
    near_result = attend_rows(
        split_heads(queries, head_count),
        split_heads(key_vectors, head_count),
        split_heads(value_vectors, head_count),
        visible,
    )
    far_result = attend_rows(
        split_heads(moved_queries, head_count),
        split_heads(moved_keys, head_count),
        split_heads(moved_values, head_count),
        visible,
    )
    returned = to_frames(far_result.reshape(row_count, row_width), frames, group_size)[inverse]
    per_head = jnp.where(temporal, split_heads(returned, head_count), near_result)
    attended = per_head.reshape(row_count, row_width)
    head_columns = lax.all_gather(attended, "mlp", axis=1, tiled=True)
    projected = jnp.dot(
        head_columns,
        lax.all_gather(out_weight, "seq", axis=0, tiled=True),
        preferred_element_type=jnp.float32,
    )
    return (gate_values[None, :] * projected).astype(jnp.bfloat16)


PLANE = 4
MESH = pl.DeviceIdType.MESH


def aligned(index, size):
    return pl.ds(pl.multiple_of(index * size, size), size)


def branch_kernel(
    frames, slots, depth,
    heads_ref, kinds_ref, bias_ref, order_ref, q_ref, k_ref, v_ref, w_ref, gate_ref,
    out_ref,
    packed, moved, result, returned, attended, w_rows, w_slots, part_out, part_own, part_in,
    done_out, done,
    qkv_send, qkv_recv, res_send, res_recv, near_send, near_recv, far_send, far_recv,
    w1_send, w1_recv, w1_own, w2_send, w2_recv, p_send, p_recv, o_send, o_recv,
):
    rows, width = q_ref.shape
    heads = width // depth
    group = rows // frames
    layers = frames // PLANE
    half_layers = layers // 2
    w_part, columns = w_ref.shape[0], width // PLANE
    me, m = lax.axis_index("seq"), lax.axis_index("mlp")
    z, p = me // PLANE, me % PLANE
    scale = 1.0 / math.sqrt(depth)
    bf16, f32 = jnp.bfloat16, jnp.float32

    def remote(src, dst, send, recv, seq, mlp):
        return pltpu.make_async_remote_copy(
            src_ref=src, dst_ref=dst, send_sem=send, recv_sem=recv,
            device_id=(seq, mlp), device_id_type=MESH,
        )

    barrier = pltpu.get_barrier_semaphore()
    for d in range(frames):
        peer = (me + d) % frames
        if d:
            pl.semaphore_signal(barrier, inc=1, device_id=(peer, m), device_id_type=MESH)
        pl.semaphore_signal(barrier, inc=1, device_id=(peer, 1 - m), device_id_type=MESH)

    places = lax.broadcasted_iota(jnp.int32, (rows, rows), 0)
    back_f32 = jnp.where(places == order_ref[...], 1.0, 0.0)
    back = back_f32.astype(bf16)
    forth = back_f32.T.astype(bf16)

    def head_of(t):
        return t if slots == heads else heads_ref[t]

    def pack(t, carry):
        h = head_of(t)
        for i, ref in enumerate((q_ref, k_ref, v_ref)):
            block = jnp.dot(forth, ref[:, aligned(h, depth)], preferred_element_type=f32)
            packed[:, :, aligned(3 * t + i, depth)] = block.astype(bf16).reshape(frames, group, depth)
        return carry

    lax.fori_loop(0, slots, pack, 0)
    pl.semaphore_wait(barrier, 2 * frames - 1)

    def qkv_copy(d, to, slot):
        return remote(packed.at[to], moved.at[slot], qkv_send.at[d], qkv_recv.at[d], to, m)

    for d in range(1, frames):
        qkv_copy(d, (me + d) % frames, me).start()
    moved[me] = packed[me]

    core = z // half_layers
    layer = z % half_layers

    def w1_copy(d, to, source, source_m):
        return remote(
            w_ref.at[:, aligned(to, columns)],
            w_rows.at[source_m, aligned(layer * PLANE + source, w_part), :],
            w1_send.at[d], w1_recv.at[d, source_m], z * PLANE + to, core,
        )

    for d in range(1, PLANE):
        w1_copy(d, (p + d) % PLANE, p, m).start()

    @pl.when(m != core)
    def _():
        w1_copy(0, p, p, m).start()

    own_copy = pltpu.make_async_copy(
        w_ref.at[:, aligned(p, columns)],
        w_rows.at[m, aligned(layer * PLANE + p, w_part), :],
        w1_own,
    )

    @pl.when(m == core)
    def _():
        own_copy.start()

    row_ids = lax.broadcasted_iota(jnp.int32, (rows, rows), 0)
    col_ids = lax.broadcasted_iota(jnp.int32, (rows, rows), 1)
    block = rows // 2
    part = block // frames
    assert 2 * block == rows and 2 * part == group

    def attend(q, k, v, t, row_block, col_block):
        levels = bias_ref[t]
        levels = jnp.concatenate([levels, levels], axis=1)
        first = col_block[0:1] == 0
        upper = jnp.where(first, levels[0:1], levels[1:2])
        lower = jnp.where(first, levels[2:3], levels[3:4])
        bias = jnp.where(row_block == 0, upper, lower)
        scores = lax.dot_general(q, k, (((1,), (1,)), ((), ())), preferred_element_type=f32)
        scores = scores * scale + bias
        weights = jnp.exp(scores - jnp.max(scores, axis=1, keepdims=True))
        total = jnp.sum(weights, axis=1, keepdims=True)
        mixed = jnp.dot(weights.astype(bf16), v, preferred_element_type=f32)
        return (mixed / total).astype(bf16)

    def near_head(t, carry):
        at = aligned(head_of(t), depth)
        attended[p, :, aligned(t, depth)] = attend(
            q_ref[:, at], k_ref[:, at], v_ref[:, at], t, row_ids // block, col_ids // block
        )
        return carry

    far_cols, near_cols = pl.ds(0, slots * depth), pl.ds(slots * depth, (heads - slots) * depth)

    def near_copy(d, to, source):
        ref = attended.at[source, :, near_cols]
        return remote(ref, ref, near_send.at[d], near_recv.at[d], z * PLANE + to, m)

    def far_copy(d, to, source):
        ref = attended.at[source, :, far_cols]
        return remote(ref, ref, far_send.at[d], far_recv.at[d], z * PLANE + to, m)

    if slots < heads:
        lax.fori_loop(slots, heads, near_head, 0)
        for d in range(1, PLANE):
            near_copy(d, (p + d) % PLANE, p).start()
    lax.fori_loop(0, slots, near_head, 0)

    @pl.when(m != core)
    def _():
        w1_copy(0, p, p, m).wait_send()

    @pl.when(m == core)
    def _():
        own_copy.wait()
        for d in range(PLANE):
            source = (p + PLANE - d) % PLANE
            if d:
                w1_copy(d, p, source, m).wait_recv()
            w1_copy(d, p, source, 1 - m).wait_recv()

    for d in range(1, PLANE):
        w1_copy(d, (p + d) % PLANE, p, m).wait_send()

    def line_copy(b, way, to):
        ref = w_rows.at[:, pl.ds(b * PLANE * w_part, PLANE * w_part), :]
        return remote(ref, ref, w2_send.at[b, way], w2_recv.at[b], to * PLANE + p, m)

    def line_round(step):
        for b in range(half_layers):
            distance = z - (m * half_layers + b)
            if step:
                @pl.when(jnp.logical_or(distance == step, distance == -step))
                def _():
                    line_copy(b, 0, z).wait_recv()

            @pl.when(jnp.logical_and(distance == step, z < layers - 1))
            def _():
                line_copy(b, 0, z + 1).start()

            @pl.when(jnp.logical_and(distance == -step, z > 0))
            def _():
                line_copy(b, 1, z - 1).start()

    def line_end():
        for b in range(half_layers):
            distance = z - (m * half_layers + b)

            @pl.when(jnp.logical_and(distance >= 0, z < layers - 1))
            def _():
                line_copy(b, 0, z).wait_send()

            @pl.when(jnp.logical_and(distance <= 0, z > 0))
            def _():
                line_copy(b, 1, z).wait_send()

    for d in range(1, frames):
        qkv_copy(d, me, (me + frames - d) % frames).wait_recv()
    line_round(0)

    def far_head(t, carry):
        q, k, v = (moved[:, :, aligned(3 * t + i, depth)].reshape(rows, depth) for i in range(3))
        mixed = attend(q, k, v, t, (row_ids % group) // part, (col_ids % group) // part)
        result[:, :, aligned(t, depth)] = mixed.reshape(frames, group, depth)
        return carry

    lax.fori_loop(0, slots, far_head, 0)

    def res_copy(d, to, slot):
        return remote(result.at[to], returned.at[slot], res_send.at[d], res_recv.at[d], to, m)

    for d in range(1, frames):
        res_copy(d, (me + d) % frames, me).start()
    returned[me] = result[me]
    line_round(1)
    for d in range(1, frames):
        res_copy(d, me, (me + frames - d) % frames).wait_recv()

    def unpack(t, carry):
        at = aligned(t, depth)
        rows_back = jnp.dot(back, returned[:, :, at].reshape(rows, depth), preferred_element_type=f32)
        temporal = kinds_ref[:, at] == 1
        attended[p, :, at] = jnp.where(temporal, rows_back, attended[p, :, at].astype(f32)).astype(bf16)
        return carry

    lax.fori_loop(0, slots, unpack, 0)
    for d in range(1, PLANE):
        far_copy(d, (p + d) % PLANE, p).start()
    for step in range(2, layers):
        line_round(step)
    line_end()

    def order_rows(t, carry):
        at = aligned(t, depth)
        source = aligned(head_of(t), depth)
        w_slots[0, at, :] = w_rows[0, source, :]
        w_slots[1, at, :] = w_rows[1, source, :]
        return carry

    lax.fori_loop(0, heads, order_rows, 0)

    def part_copy(d):
        return remote(part_out.at[d], part_in.at[d], p_send.at[d], p_recv.at[d], me, 1 - m)

    for d in range(PLANE):
        source = (p + PLANE - d) % PLANE
        if d:
            if slots < heads:
                near_copy(d, p, source).wait_recv()
            far_copy(d, p, source).wait_recv()
        rows_in = attended[source]
        part_out[d] = jnp.dot(rows_in, w_slots[1 - m], preferred_element_type=f32)
        part_copy(d).start()
        part_own[d] = jnp.dot(rows_in, w_slots[m], preferred_element_type=f32)

    gate = gate_ref[:, aligned(p, columns)]

    def done_copy(d, to, source):
        return remote(
            done_out.at[d], done.at[:, aligned(source, columns)],
            o_send.at[d], o_recv.at[d], z * PLANE + to, m,
        )

    for d in range(PLANE):
        part_copy(d).wait_recv()
        gated = (gate * (part_own[d] + part_in[d])).astype(bf16)
        if d:
            done_out[d] = gated
            done_copy(d, (p + PLANE - d) % PLANE, p).start()
        else:
            done[:, aligned(p, columns)] = gated
    for d in range(1, frames):
        qkv_copy(d, (me + d) % frames, me).wait_send()
        res_copy(d, (me + d) % frames, me).wait_send()
    for d in range(PLANE):
        part_copy(d).wait_send()
    for d in range(1, PLANE):
        if slots < heads:
            near_copy(d, (p + d) % PLANE, p).wait_send()
        far_copy(d, (p + d) % PLANE, p).wait_send()
        done_copy(d, (p + PLANE - d) % PLANE, p).wait_send()
        done_copy(d, p, (p + d) % PLANE).wait_recv()
    out_ref[...] = done[...]


def branch_call(frames, slots, head_order, slot_kinds, slot_bias, order_map, q, k, v, w, gate):
    rows, width = q.shape
    heads = slot_bias.shape[0]
    depth = width // heads
    group, columns = rows // frames, width // PLANE
    half = w.shape[0] * frames // 2
    half_layers = frames // PLANE // 2
    bf16, f32, dma = jnp.bfloat16, jnp.float32, pltpu.SemaphoreType.DMA
    smem, vmem = pl.BlockSpec(memory_space=pltpu.SMEM), pl.BlockSpec(memory_space=pltpu.VMEM)
    return pl.pallas_call(
        functools.partial(branch_kernel, frames, slots, depth),
        out_shape=jax.ShapeDtypeStruct((rows, width), bf16),
        in_specs=[smem] + [vmem] * 8,
        out_specs=vmem,
        scratch_shapes=[
            pltpu.VMEM((frames, group, 3 * slots * depth), bf16),
            pltpu.VMEM((frames, group, 3 * slots * depth), bf16),
            pltpu.VMEM((frames, group, slots * depth), bf16),
            pltpu.VMEM((frames, group, slots * depth), bf16),
            pltpu.VMEM((PLANE, rows, width), bf16),
            pltpu.VMEM((2, half, columns), bf16),
            pltpu.VMEM((2, half, columns), bf16),
            pltpu.VMEM((PLANE, rows, columns), f32),
            pltpu.VMEM((PLANE, rows, columns), f32),
            pltpu.VMEM((PLANE, rows, columns), f32),
            pltpu.VMEM((PLANE, rows, columns), bf16),
            pltpu.VMEM((rows, width), bf16),
            dma((frames,)), dma((frames,)), dma((frames,)), dma((frames,)),
            dma((PLANE,)), dma((PLANE,)), dma((PLANE,)), dma((PLANE,)),
            dma((PLANE,)), dma((PLANE, 2)), dma(()), dma((half_layers, 2)), dma((half_layers,)),
            dma((PLANE,)), dma((PLANE,)), dma((PLANE,)), dma((PLANE,)),
        ],
        compiler_params=pltpu.CompilerParams(
            collective_id=slots, has_side_effects=True, vmem_limit_bytes=48 * 2**20
        ),
        name="branch_%d" % slots,
    )(
        head_order, slot_kinds, slot_bias, order_map.reshape(1, rows),
        q, k, v, w, gate.reshape(1, width),
    )


def fused_local(q, k, v, head_kinds, block_masks, order_map, out_weight, gate_values):
    frames = lax.axis_size("seq")
    heads = head_kinds.shape[0]
    depth = q.shape[1] // heads
    bias = jnp.where(block_masks == 1, 0.0, -1e30).reshape(heads, 4)

    def call(slots, order, kinds, bias):
        return branch_call(
            frames, slots, order, jnp.repeat(kinds, depth)[None, :],
            jnp.broadcast_to(bias[:, :, None], (heads, 4, depth)),
            order_map, q, k, v, out_weight, gate_values,
        )

    return call(heads, jnp.arange(heads, dtype=jnp.int32), head_kinds, bias)


def fits(mesh):
    frames = mesh.shape["seq"]
    return mesh.shape["mlp"] == 2 and frames % (2 * PLANE) == 0 and frames <= 16


def solution(mesh):
    in_specs = (
        P("seq", "mlp"),
        P("seq", "mlp"),
        P("seq", "mlp"),
        P("mlp"),
        P("mlp", None, None),
        P(),
        P("seq", "mlp"),
        P("mlp"),
    )
    out_specs = P("seq", "mlp")
    body = fused_local if fits(mesh) else local
    return jax.shard_map(body, mesh=mesh, in_specs=in_specs, out_specs=out_specs, check_vma=False)
```

```python
import functools
import math

import jax
import jax.numpy as jnp
from jax import lax
from jax.experimental import pallas as pl
from jax.experimental.pallas import tpu as pltpu
from jax.sharding import PartitionSpec as P


def attend_rows(query_rows, key_rows, value_rows, visible):
    row_count, head_count, head_depth = query_rows.shape
    score_scale = 1.0 / math.sqrt(head_depth)
    scores = (
        jnp.einsum("qhd,khd->hqk", query_rows, key_rows, preferred_element_type=jnp.float32)
        * score_scale
    )
    row_max = jnp.max(jnp.where(visible, scores, -jnp.inf), axis=2, keepdims=True)
    weights = jnp.where(visible, jnp.exp(scores - row_max), 0.0)
    row_total = jnp.sum(weights, axis=2)
    combined = jnp.einsum(
        "hqk,khd->qhd", weights.astype(jnp.bfloat16), value_rows, preferred_element_type=jnp.float32
    )
    outputs = (combined / jnp.transpose(row_total)[:, :, None]).astype(jnp.bfloat16)
    return outputs


def to_positions(query_rows, key_rows, value_rows, frames, group_size):
    row_width = query_rows.shape[1]
    exchanged = (
        lax.all_to_all(
            query_rows.reshape(frames, group_size, 1, row_width),
            "seq",
            split_axis=0,
            concat_axis=2,
            tiled=True,
        ),
        lax.all_to_all(
            key_rows.reshape(frames, group_size, 1, row_width),
            "seq",
            split_axis=0,
            concat_axis=2,
            tiled=True,
        ),
        lax.all_to_all(
            value_rows.reshape(frames, group_size, 1, row_width),
            "seq",
            split_axis=0,
            concat_axis=2,
            tiled=True,
        ),
    )
    return tuple((member.reshape(group_size * frames, row_width) for member in exchanged))


def to_frames(results, frames, group_size):
    row_width = results.shape[1]
    exchanged = lax.all_to_all(
        results.reshape(1, group_size, frames, row_width),
        "seq",
        split_axis=2,
        concat_axis=0,
        tiled=True,
    )
    return exchanged.reshape(frames * group_size, row_width)


def split_heads(array, head_count):
    return array.reshape(array.shape[0], head_count, array.shape[1] // head_count)


def local(
    queries, key_vectors, value_vectors, head_kinds, block_masks, order_map, out_weight, gate_values
):
    row_count, row_width = queries.shape
    head_count = head_kinds.shape[0]
    frames = lax.axis_size("seq")
    group_size = row_count // frames
    block_size = row_count // block_masks.shape[1]
    inverse = (
        jnp.zeros((row_count,), jnp.int32).at[order_map].set(jnp.arange(row_count, dtype=jnp.int32))
    )
    visible = jnp.repeat(jnp.repeat(block_masks == 1, block_size, axis=1), block_size, axis=2)
    temporal = (head_kinds == 1)[None, :, None]
    moved_queries, moved_keys, moved_values = to_positions(
        queries[order_map], key_vectors[order_map], value_vectors[order_map], frames, group_size
    )
    near_result = attend_rows(
        split_heads(queries, head_count),
        split_heads(key_vectors, head_count),
        split_heads(value_vectors, head_count),
        visible,
    )
    far_result = attend_rows(
        split_heads(moved_queries, head_count),
        split_heads(moved_keys, head_count),
        split_heads(moved_values, head_count),
        visible,
    )
    returned = to_frames(far_result.reshape(row_count, row_width), frames, group_size)[inverse]
    per_head = jnp.where(temporal, split_heads(returned, head_count), near_result)
    attended = per_head.reshape(row_count, row_width)
    head_columns = lax.all_gather(attended, "mlp", axis=1, tiled=True)
    projected = jnp.dot(
        head_columns,
        lax.all_gather(out_weight, "seq", axis=0, tiled=True),
        preferred_element_type=jnp.float32,
    )
    return (gate_values[None, :] * projected).astype(jnp.bfloat16)


PLANE = 4
MESH = pl.DeviceIdType.MESH


def aligned(index, size):
    return pl.ds(pl.multiple_of(index * size, size), size)


def branch_kernel(
    frames, slots, depth,
    heads_ref, kinds_hbm, bias_hbm, order_hbm, q_hbm, k_hbm, v_hbm, w_ref, gate_hbm,
    out_ref,
    kinds_ref, bias_ref, order_ref, q_ref, k_ref, v_ref, gate_ref, fetch_sem, head_sem,
    packed, moved, result, returned, attended, w_rows, w_slots, part_out, part_own, part_in,
    done_out, done,
    qkv_send, qkv_recv, res_send, res_recv, near_send, near_recv, far_send, far_recv,
    w1_send, w1_recv, w1_own, w2_send, w2_recv, p_send, p_recv, o_send, o_recv,
):
    rows, width = q_hbm.shape
    heads = width // depth
    group = rows // frames
    layers = frames // PLANE
    half_layers = layers // 2
    w_part, unit = w_ref.shape[:2]
    pieces, columns = depth // unit, width // PLANE
    me, m = lax.axis_index("seq"), lax.axis_index("mlp")
    z, p = me // PLANE, me % PLANE
    scale = 1.0 / math.sqrt(depth)
    bf16, f32 = jnp.bfloat16, jnp.float32

    def remote(src, dst, send, recv, seq, mlp):
        return pltpu.make_async_remote_copy(
            src_ref=src, dst_ref=dst, send_sem=send, recv_sem=recv,
            device_id=(seq, mlp), device_id_type=MESH,
        )

    fetches = [
        pltpu.make_async_copy(src, dst, fetch_sem.at[i])
        for i, (src, dst) in enumerate((
            (order_hbm, order_ref), (bias_hbm, bias_ref), (kinds_hbm, kinds_ref), (gate_hbm, gate_ref),
        ))
    ] + [
        pltpu.make_async_copy(src.at[:, pl.ds(h * depth, depth)], dst.at[h], head_sem.at[i, h])
        for i, (src, dst) in enumerate(((q_hbm, q_ref), (k_hbm, k_ref), (v_hbm, v_ref)))
        for h in range(heads)
    ]
    for fetch in fetches:
        fetch.start()
    barrier = pltpu.get_barrier_semaphore()
    for d in range(frames):
        peer = (me + d) % frames
        if d:
            pl.semaphore_signal(barrier, inc=1, device_id=(peer, m), device_id_type=MESH)
        pl.semaphore_signal(barrier, inc=1, device_id=(peer, 1 - m), device_id_type=MESH)

    for fetch in fetches:
        fetch.wait()

    places = lax.broadcasted_iota(jnp.int32, (rows, rows), 0)
    back_f32 = jnp.where(places == order_ref[...], 1.0, 0.0)
    back = back_f32.astype(bf16)
    forth = back_f32.T.astype(bf16)

    def head_of(t):
        return t if slots == heads else heads_ref[t]

    def pack(t, carry):
        h = head_of(t)
        for i, ref in enumerate((q_ref, k_ref, v_ref)):
            block = jnp.dot(forth, ref[h], preferred_element_type=f32)
            packed[:, :, aligned(3 * t + i, depth)] = block.astype(bf16).reshape(frames, group, depth)
        return carry

    lax.fori_loop(0, slots, pack, 0)
    pl.semaphore_wait(barrier, 2 * frames - 1)

    def qkv_copy(d, to, slot):
        return remote(packed.at[to], moved.at[slot], qkv_send.at[d], qkv_recv.at[d], to, m)

    for d in range(1, frames):
        qkv_copy(d, (me + d) % frames, me).start()
    moved[me] = packed[me]

    core = z // half_layers
    layer = z % half_layers

    def w1_copy(d, to, source, source_m):
        return remote(
            w_ref.at[:, :, aligned(to, columns)],
            w_rows.at[source_m, aligned(layer * PLANE + source, w_part)],
            w1_send.at[d], w1_recv.at[d, source_m], z * PLANE + to, core,
        )

    for d in range(1, PLANE):
        w1_copy(d, (p + d) % PLANE, p, m).start()

    @pl.when(m != core)
    def _():
        w1_copy(0, p, p, m).start()

    own_copy = pltpu.make_async_copy(
        w_ref.at[:, :, aligned(p, columns)],
        w_rows.at[m, aligned(layer * PLANE + p, w_part)],
        w1_own,
    )

    @pl.when(m == core)
    def _():
        own_copy.start()

    row_ids = lax.broadcasted_iota(jnp.int32, (rows, rows), 0)
    col_ids = lax.broadcasted_iota(jnp.int32, (rows, rows), 1)
    block = rows // 2
    part = block // frames
    assert 2 * block == rows and 2 * part == group

    def attend(q, k, v, t, row_block, col_block):
        levels = bias_ref[t]
        levels = jnp.concatenate([levels, levels], axis=1)
        first = col_block[0:1] == 0
        upper = jnp.where(first, levels[0:1], levels[1:2])
        lower = jnp.where(first, levels[2:3], levels[3:4])
        bias = jnp.where(row_block == 0, upper, lower)
        scores = lax.dot_general(q, k, (((1,), (1,)), ((), ())), preferred_element_type=f32)
        scores = scores * scale + bias
        weights = jnp.exp(scores - jnp.max(scores, axis=1, keepdims=True))
        total = jnp.sum(weights, axis=1, keepdims=True)
        mixed = jnp.dot(weights.astype(bf16), v, preferred_element_type=f32)
        return (mixed / total).astype(bf16)

    def near_head(t, carry):
        h = head_of(t)
        attended[p, :, aligned(t, depth)] = attend(
            q_ref[h], k_ref[h], v_ref[h], t, row_ids // block, col_ids // block
        )
        return carry

    far_cols, near_cols = pl.ds(0, slots * depth), pl.ds(slots * depth, (heads - slots) * depth)

    def near_copy(d, to, source):
        ref = attended.at[source, :, near_cols]
        return remote(ref, ref, near_send.at[d], near_recv.at[d], z * PLANE + to, m)

    def far_copy(d, to, source):
        ref = attended.at[source, :, far_cols]
        return remote(ref, ref, far_send.at[d], far_recv.at[d], z * PLANE + to, m)

    if slots < heads:
        lax.fori_loop(slots, heads, near_head, 0)
        for d in range(1, PLANE):
            near_copy(d, (p + d) % PLANE, p).start()
    lax.fori_loop(0, slots, near_head, 0)

    @pl.when(m != core)
    def _():
        w1_copy(0, p, p, m).wait_send()

    @pl.when(m == core)
    def _():
        own_copy.wait()
        for d in range(PLANE):
            source = (p + PLANE - d) % PLANE
            if d:
                w1_copy(d, p, source, m).wait_recv()
            w1_copy(d, p, source, 1 - m).wait_recv()

    for d in range(1, PLANE):
        w1_copy(d, (p + d) % PLANE, p, m).wait_send()

    def line_copy(b, way, to):
        ref = w_rows.at[:, pl.ds(b * PLANE * w_part, PLANE * w_part)]
        return remote(ref, ref, w2_send.at[b, way], w2_recv.at[b], to * PLANE + p, m)

    def line_round(step):
        for b in range(half_layers):
            distance = z - (m * half_layers + b)
            if step:
                @pl.when(jnp.logical_or(distance == step, distance == -step))
                def _():
                    line_copy(b, 0, z).wait_recv()

            @pl.when(jnp.logical_and(distance == step, z < layers - 1))
            def _():
                line_copy(b, 0, z + 1).start()

            @pl.when(jnp.logical_and(distance == -step, z > 0))
            def _():
                line_copy(b, 1, z - 1).start()

    def line_end():
        for b in range(half_layers):
            distance = z - (m * half_layers + b)

            @pl.when(jnp.logical_and(distance >= 0, z < layers - 1))
            def _():
                line_copy(b, 0, z).wait_send()

            @pl.when(jnp.logical_and(distance <= 0, z > 0))
            def _():
                line_copy(b, 1, z).wait_send()

    line_round(0)
    for d in range(1, frames):
        qkv_copy(d, me, (me + frames - d) % frames).wait_recv()
    line_round(1)

    def far_head(t, carry):
        q, k, v = (moved[:, :, aligned(3 * t + i, depth)].reshape(rows, depth) for i in range(3))
        mixed = attend(q, k, v, t, (row_ids % group) // part, (col_ids % group) // part)
        result[:, :, aligned(t, depth)] = mixed.reshape(frames, group, depth)
        return carry

    lax.fori_loop(0, slots, far_head, 0)

    def res_copy(d, to, slot):
        return remote(result.at[to], returned.at[slot], res_send.at[d], res_recv.at[d], to, m)

    for d in range(1, frames):
        res_copy(d, (me + d) % frames, me).start()
    returned[me] = result[me]
    for d in range(1, frames):
        res_copy(d, me, (me + frames - d) % frames).wait_recv()

    def unpack(t, carry):
        at = aligned(t, depth)
        rows_back = jnp.dot(back, returned[:, :, at].reshape(rows, depth), preferred_element_type=f32)
        temporal = kinds_ref[:, at] == 1
        attended[p, :, at] = jnp.where(temporal, rows_back, attended[p, :, at].astype(f32)).astype(bf16)
        return carry

    lax.fori_loop(0, slots, unpack, 0)
    for d in range(1, PLANE):
        far_copy(d, (p + d) % PLANE, p).start()
    for step in range(2, layers):
        line_round(step)
    line_end()

    def order_rows(t, carry):
        h = head_of(t)
        for half in range(2):
            for i in range(pieces):
                w_slots[half, aligned(t * pieces + i, unit), :] = w_rows[half, h * pieces + i]
        return carry

    lax.fori_loop(0, heads, order_rows, 0)

    def part_copy(d):
        return remote(part_out.at[d], part_in.at[d], p_send.at[d], p_recv.at[d], me, 1 - m)

    for d in range(PLANE):
        source = (p + PLANE - d) % PLANE
        if d:
            if slots < heads:
                near_copy(d, p, source).wait_recv()
            far_copy(d, p, source).wait_recv()
        rows_in = attended[source]
        part_out[d] = jnp.dot(rows_in, w_slots[1 - m], preferred_element_type=f32)
        part_copy(d).start()
        part_own[d] = jnp.dot(rows_in, w_slots[m], preferred_element_type=f32)

    gate = gate_ref[:, aligned(p, columns)]

    def done_copy(d, to, source):
        return remote(
            done_out.at[d], done.at[:, aligned(source, columns)],
            o_send.at[d], o_recv.at[d], z * PLANE + to, m,
        )

    for d in range(PLANE):
        part_copy(d).wait_recv()
        gated = (gate * (part_own[d] + part_in[d])).astype(bf16)
        if d:
            done_out[d] = gated
            done_copy(d, (p + PLANE - d) % PLANE, p).start()
        else:
            done[:, aligned(p, columns)] = gated
    for d in range(1, frames):
        qkv_copy(d, (me + d) % frames, me).wait_send()
        res_copy(d, (me + d) % frames, me).wait_send()
    for d in range(PLANE):
        part_copy(d).wait_send()
    for d in range(1, PLANE):
        if slots < heads:
            near_copy(d, (p + d) % PLANE, p).wait_send()
        far_copy(d, (p + d) % PLANE, p).wait_send()
        done_copy(d, (p + PLANE - d) % PLANE, p).wait_send()
        done_copy(d, p, (p + d) % PLANE).wait_recv()
    out_ref[...] = done[...]


def branch_call(frames, slots, head_order, slot_kinds, slot_bias, order_map, q, k, v, w, gate):
    rows, width = q.shape
    heads = slot_bias.shape[0]
    depth = width // heads
    group, columns = rows // frames, width // PLANE
    half = w.shape[0] * frames // 2
    unit = math.gcd(w.shape[0], depth)
    half_layers = frames // PLANE // 2
    bf16, f32, dma = jnp.bfloat16, jnp.float32, pltpu.SemaphoreType.DMA
    smem, vmem = pl.BlockSpec(memory_space=pltpu.SMEM), pl.BlockSpec(memory_space=pltpu.VMEM)
    return pl.pallas_call(
        functools.partial(branch_kernel, frames, slots, depth),
        out_shape=jax.ShapeDtypeStruct((rows, width), bf16),
        in_specs=[smem] + [pl.BlockSpec(memory_space=pl.ANY)] * 8,
        out_specs=vmem,
        scratch_shapes=[
            pltpu.VMEM(slot_kinds.shape, jnp.int32),
            pltpu.VMEM(slot_bias.shape, f32),
            pltpu.VMEM((1, rows), jnp.int32),
            pltpu.VMEM((heads, rows, depth), bf16),
            pltpu.VMEM((heads, rows, depth), bf16),
            pltpu.VMEM((heads, rows, depth), bf16),
            pltpu.VMEM((1, width), f32),
            dma((4,)),
            dma((3, heads)),
            pltpu.VMEM((frames, group, 3 * slots * depth), bf16),
            pltpu.VMEM((frames, group, 3 * slots * depth), bf16),
            pltpu.VMEM((frames, group, slots * depth), bf16),
            pltpu.VMEM((frames, group, slots * depth), bf16),
            pltpu.VMEM((PLANE, rows, width), bf16),
            pltpu.VMEM((2, half // unit, unit, columns), bf16),
            pltpu.VMEM((2, half, columns), bf16),
            pltpu.VMEM((PLANE, rows, columns), f32),
            pltpu.VMEM((PLANE, rows, columns), f32),
            pltpu.VMEM((PLANE, rows, columns), f32),
            pltpu.VMEM((PLANE, rows, columns), bf16),
            pltpu.VMEM((rows, width), bf16),
            dma((frames,)), dma((frames,)), dma((frames,)), dma((frames,)),
            dma((PLANE,)), dma((PLANE,)), dma((PLANE,)), dma((PLANE,)),
            dma((PLANE,)), dma((PLANE, 2)), dma(()), dma((half_layers, 2)), dma((half_layers,)),
            dma((PLANE,)), dma((PLANE,)), dma((PLANE,)), dma((PLANE,)),
        ],
        compiler_params=pltpu.CompilerParams(
            collective_id=slots, has_side_effects=True, vmem_limit_bytes=48 * 2**20
        ),
        name="branch_%d" % slots,
    )(
        head_order, slot_kinds, slot_bias, order_map.reshape(1, rows),
        q, k, v, w.reshape(-1, unit, width), gate.reshape(1, width),
    )


def count_kernel(kinds_ref, most_ref, other, send, recv):
    me, m = lax.axis_index("seq"), lax.axis_index("mlp")
    barrier = pltpu.get_barrier_semaphore()
    pl.semaphore_signal(barrier, inc=1, device_id=(me, 1 - m), device_id_type=MESH)
    pl.semaphore_wait(barrier, 1)
    copy = pltpu.make_async_remote_copy(
        src_ref=kinds_ref, dst_ref=other, send_sem=send, recv_sem=recv,
        device_id=(me, 1 - m), device_id_type=MESH,
    )
    copy.start()
    copy.wait()
    counts = [jnp.sum(ref[...], axis=1, keepdims=True) for ref in (kinds_ref, other)]
    most_ref[...] = jnp.broadcast_to(jnp.maximum(*counts), most_ref.shape)


def most_temporal(head_kinds):
    vmem, dma = pl.BlockSpec(memory_space=pltpu.VMEM), pltpu.SemaphoreType.DMA
    kinds = jnp.zeros((8, 128), jnp.int32).at[0, : head_kinds.shape[0]].set(head_kinds)
    return pl.pallas_call(
        count_kernel,
        out_shape=jax.ShapeDtypeStruct((8, 128), jnp.int32),
        in_specs=[vmem],
        out_specs=vmem,
        scratch_shapes=[pltpu.VMEM((8, 128), jnp.int32), dma(()), dma(())],
        compiler_params=pltpu.CompilerParams(collective_id=64, has_side_effects=True),
        name="count_temporal",
    )(kinds)[0, 0]


def fused_local(q, k, v, head_kinds, block_masks, order_map, out_weight, gate_values):
    frames = lax.axis_size("seq")
    heads = head_kinds.shape[0]
    depth = q.shape[1] // heads
    sizes = [heads // 2, heads // 2 + 1, heads // 2 + 2, heads // 2 + 3]
    most = most_temporal(head_kinds)
    branch = sum((most > size).astype(jnp.int32) for size in sizes)

    ids = jnp.arange(heads, dtype=jnp.int32)
    near_kinds = 1 - head_kinds
    ahead = ids[None, :] < ids[:, None]
    count = jnp.sum(head_kinds)
    far_rank = jnp.sum(jnp.where(ahead, head_kinds[None, :], 0), axis=1)
    near_rank = jnp.sum(jnp.where(ahead, near_kinds[None, :], 0), axis=1)
    slot = jnp.where(head_kinds == 1, far_rank, count + near_rank)
    chosen = slot[None, :] == ids[:, None]
    order = jnp.sum(jnp.where(chosen, ids[None, :], 0), axis=1)
    bias = jnp.where(block_masks == 1, 0.0, -1e30).reshape(heads, 4)
    slot_bias = jnp.sum(jnp.where(chosen[:, :, None], bias[None, :, :], 0.0), axis=1)
    spread = lambda kinds: jnp.repeat(kinds, depth)[None, :]
    widen = lambda levels: jnp.broadcast_to(levels[:, :, None], (heads, 4, depth))

    def call(slots, order, kinds, bias):
        return branch_call(
            frames, slots, order, spread(kinds), widen(bias),
            order_map, q, k, v, out_weight, gate_values,
        )

    branches = [
        functools.partial(call, size, order, (ids < count).astype(jnp.int32), slot_bias) for size in sizes
    ]
    branches.append(functools.partial(call, heads, ids, head_kinds, bias))
    return lax.switch(branch, branches)


def fits(mesh):
    frames = mesh.shape["seq"]
    return mesh.shape["mlp"] == 2 and frames % (2 * PLANE) == 0 and frames <= 16


def solution(mesh):
    in_specs = (
        P("seq", "mlp"),
        P("seq", "mlp"),
        P("seq", "mlp"),
        P("mlp"),
        P("mlp", None, None),
        P(),
        P("seq", "mlp"),
        P("mlp"),
    )
    out_specs = P("seq", "mlp")
    body = fused_local if fits(mesh) else local
    return jax.shard_map(body, mesh=mesh, in_specs=in_specs, out_specs=out_specs, check_vma=False)
```

```python
import functools
import math

import jax
import jax.numpy as jnp
from jax import lax
from jax.experimental import pallas as pl
from jax.experimental.pallas import tpu as pltpu
from jax.sharding import PartitionSpec as P


def attend_rows(query_rows, key_rows, value_rows, visible):
    row_count, head_count, head_depth = query_rows.shape
    score_scale = 1.0 / math.sqrt(head_depth)
    scores = (
        jnp.einsum("qhd,khd->hqk", query_rows, key_rows, preferred_element_type=jnp.float32)
        * score_scale
    )
    row_max = jnp.max(jnp.where(visible, scores, -jnp.inf), axis=2, keepdims=True)
    weights = jnp.where(visible, jnp.exp(scores - row_max), 0.0)
    row_total = jnp.sum(weights, axis=2)
    combined = jnp.einsum(
        "hqk,khd->qhd", weights.astype(jnp.bfloat16), value_rows, preferred_element_type=jnp.float32
    )
    outputs = (combined / jnp.transpose(row_total)[:, :, None]).astype(jnp.bfloat16)
    return outputs


def to_positions(query_rows, key_rows, value_rows, frames, group_size):
    row_width = query_rows.shape[1]
    exchanged = (
        lax.all_to_all(
            query_rows.reshape(frames, group_size, 1, row_width),
            "seq",
            split_axis=0,
            concat_axis=2,
            tiled=True,
        ),
        lax.all_to_all(
            key_rows.reshape(frames, group_size, 1, row_width),
            "seq",
            split_axis=0,
            concat_axis=2,
            tiled=True,
        ),
        lax.all_to_all(
            value_rows.reshape(frames, group_size, 1, row_width),
            "seq",
            split_axis=0,
            concat_axis=2,
            tiled=True,
        ),
    )
    return tuple((member.reshape(group_size * frames, row_width) for member in exchanged))


def to_frames(results, frames, group_size):
    row_width = results.shape[1]
    exchanged = lax.all_to_all(
        results.reshape(1, group_size, frames, row_width),
        "seq",
        split_axis=2,
        concat_axis=0,
        tiled=True,
    )
    return exchanged.reshape(frames * group_size, row_width)


def split_heads(array, head_count):
    return array.reshape(array.shape[0], head_count, array.shape[1] // head_count)


def local(
    queries, key_vectors, value_vectors, head_kinds, block_masks, order_map, out_weight, gate_values
):
    row_count, row_width = queries.shape
    head_count = head_kinds.shape[0]
    frames = lax.axis_size("seq")
    group_size = row_count // frames
    block_size = row_count // block_masks.shape[1]
    inverse = (
        jnp.zeros((row_count,), jnp.int32).at[order_map].set(jnp.arange(row_count, dtype=jnp.int32))
    )
    visible = jnp.repeat(jnp.repeat(block_masks == 1, block_size, axis=1), block_size, axis=2)
    temporal = (head_kinds == 1)[None, :, None]
    moved_queries, moved_keys, moved_values = to_positions(
        queries[order_map], key_vectors[order_map], value_vectors[order_map], frames, group_size
    )
    near_result = attend_rows(
        split_heads(queries, head_count),
        split_heads(key_vectors, head_count),
        split_heads(value_vectors, head_count),
        visible,
    )
    far_result = attend_rows(
        split_heads(moved_queries, head_count),
        split_heads(moved_keys, head_count),
        split_heads(moved_values, head_count),
        visible,
    )
    returned = to_frames(far_result.reshape(row_count, row_width), frames, group_size)[inverse]
    per_head = jnp.where(temporal, split_heads(returned, head_count), near_result)
    attended = per_head.reshape(row_count, row_width)
    head_columns = lax.all_gather(attended, "mlp", axis=1, tiled=True)
    projected = jnp.dot(
        head_columns,
        lax.all_gather(out_weight, "seq", axis=0, tiled=True),
        preferred_element_type=jnp.float32,
    )
    return (gate_values[None, :] * projected).astype(jnp.bfloat16)


PLANE = 4
MESH = pl.DeviceIdType.MESH


def aligned(index, size):
    return pl.ds(pl.multiple_of(index * size, size), size)


def slot_chunks(slots):
    parts = max(1, min(4, slots // 2))
    edges = [slots * i // parts for i in range(parts + 1)]
    return list(zip(edges[:-1], edges[1:]))


def branch_kernel(
    frames, slots, depth,
    heads_ref, kinds_hbm, bias_hbm, order_hbm, q_hbm, k_hbm, v_hbm, w_ref, gate_hbm,
    out_ref,
    kinds_ref, bias_ref, order_ref, q_ref, k_ref, v_ref, gate_ref, fetch_sem, head_sem,
    packed, moved, result, returned, attended, w_rows, w_slots, part_out, part_own, part_in,
    done_out, done,
    qkv_send, qkv_recv, res_send, res_recv, near_send, near_recv, far_send, far_recv,
    w1_send, w1_recv, w1_own, w2_send, w2_recv, p_send, p_recv, o_send, o_recv,
):
    rows, width = q_hbm.shape
    heads = width // depth
    group = rows // frames
    layers = frames // PLANE
    half_layers = layers // 2
    w_part, unit = w_ref.shape[:2]
    pieces, columns = depth // unit, width // PLANE
    me, m = lax.axis_index("seq"), lax.axis_index("mlp")
    z, p = me // PLANE, me % PLANE
    scale = 1.0 / math.sqrt(depth)
    bf16, f32 = jnp.bfloat16, jnp.float32

    def remote(src, dst, send, recv, seq, mlp):
        return pltpu.make_async_remote_copy(
            src_ref=src, dst_ref=dst, send_sem=send, recv_sem=recv,
            device_id=(seq, mlp), device_id_type=MESH,
        )

    fetches = [
        pltpu.make_async_copy(src, dst, fetch_sem.at[i])
        for i, (src, dst) in enumerate((
            (order_hbm, order_ref), (bias_hbm, bias_ref), (kinds_hbm, kinds_ref), (gate_hbm, gate_ref),
        ))
    ] + [
        pltpu.make_async_copy(src.at[:, pl.ds(h * depth, depth)], dst.at[h], head_sem.at[i, h])
        for i, (src, dst) in enumerate(((q_hbm, q_ref), (k_hbm, k_ref), (v_hbm, v_ref)))
        for h in range(heads)
    ]
    for fetch in fetches:
        fetch.start()
    barrier = pltpu.get_barrier_semaphore()
    for d in range(frames):
        peer = (me + d) % frames
        if d:
            pl.semaphore_signal(barrier, inc=1, device_id=(peer, m), device_id_type=MESH)
        pl.semaphore_signal(barrier, inc=1, device_id=(peer, 1 - m), device_id_type=MESH)

    for fetch in fetches:
        fetch.wait()

    places = lax.broadcasted_iota(jnp.int32, (rows, rows), 0)
    back_f32 = jnp.where(places == order_ref[...], 1.0, 0.0)
    back = back_f32.astype(bf16)
    forth = back_f32.T.astype(bf16)

    def head_of(t):
        return t if slots == heads else heads_ref[t]

    def pack(t, carry):
        h = head_of(t)
        for i, ref in enumerate((q_ref, k_ref, v_ref)):
            block = jnp.dot(forth, ref[h], preferred_element_type=f32)
            packed[:, :, aligned(3 * t + i, depth)] = block.astype(bf16).reshape(frames, group, depth)
        return carry

    chunks = slot_chunks(slots)

    def qkv_copy(c, d, to, slot):
        first, last = chunks[c]
        lanes = pl.ds(3 * first * depth, 3 * (last - first) * depth)
        return remote(
            packed.at[to, :, lanes], moved.at[slot, :, lanes],
            qkv_send.at[c, d], qkv_recv.at[c, d], to, m,
        )

    for c, (first, last) in enumerate(chunks):
        lax.fori_loop(first, last, pack, 0)
        if c == 0:
            pl.semaphore_wait(barrier, 2 * frames - 1)
        for d in range(1, frames):
            qkv_copy(c, d, (me + d) % frames, me).start()
    moved[me] = packed[me]

    core = z // half_layers
    layer = z % half_layers

    def w1_copy(d, to, source, source_m):
        return remote(
            w_ref.at[:, :, aligned(to, columns)],
            w_rows.at[source_m, aligned(layer * PLANE + source, w_part)],
            w1_send.at[d], w1_recv.at[d, source_m], z * PLANE + to, core,
        )

    for d in range(1, PLANE):
        w1_copy(d, (p + d) % PLANE, p, m).start()

    @pl.when(m != core)
    def _():
        w1_copy(0, p, p, m).start()

    own_copy = pltpu.make_async_copy(
        w_ref.at[:, :, aligned(p, columns)],
        w_rows.at[m, aligned(layer * PLANE + p, w_part)],
        w1_own,
    )

    @pl.when(m == core)
    def _():
        own_copy.start()

    row_ids = lax.broadcasted_iota(jnp.int32, (rows, rows), 0)
    col_ids = lax.broadcasted_iota(jnp.int32, (rows, rows), 1)
    block = rows // 2
    part = block // frames
    assert 2 * block == rows and 2 * part == group

    def attend(q, k, v, t, row_block, col_block):
        levels = bias_ref[t]
        levels = jnp.concatenate([levels, levels], axis=1)
        first = col_block[0:1] == 0
        upper = jnp.where(first, levels[0:1], levels[1:2])
        lower = jnp.where(first, levels[2:3], levels[3:4])
        bias = jnp.where(row_block == 0, upper, lower)
        scores = lax.dot_general(q, k, (((1,), (1,)), ((), ())), preferred_element_type=f32)
        scores = scores * scale + bias
        weights = jnp.exp(scores - jnp.max(scores, axis=1, keepdims=True))
        total = jnp.sum(weights, axis=1, keepdims=True)
        mixed = jnp.dot(weights.astype(bf16), v, preferred_element_type=f32)
        return (mixed / total).astype(bf16)

    def near_head(t, carry):
        h = head_of(t)
        attended[p, :, aligned(t, depth)] = attend(
            q_ref[h], k_ref[h], v_ref[h], t, row_ids // block, col_ids // block
        )
        return carry

    near_cols = pl.ds(slots * depth, (heads - slots) * depth)

    def near_copy(d, to, source):
        ref = attended.at[source, :, near_cols]
        return remote(ref, ref, near_send.at[d], near_recv.at[d], z * PLANE + to, m)

    def far_copy(c, d, to, source):
        first, last = chunks[c]
        ref = attended.at[source, :, pl.ds(first * depth, (last - first) * depth)]
        return remote(ref, ref, far_send.at[c, d], far_recv.at[c, d], z * PLANE + to, m)

    if slots < heads:
        lax.fori_loop(slots, heads, near_head, 0)
        for d in range(1, PLANE):
            near_copy(d, (p + d) % PLANE, p).start()
    lax.fori_loop(0, slots, near_head, 0)

    @pl.when(m != core)
    def _():
        w1_copy(0, p, p, m).wait_send()

    @pl.when(m == core)
    def _():
        own_copy.wait()
        for d in range(PLANE):
            source = (p + PLANE - d) % PLANE
            if d:
                w1_copy(d, p, source, m).wait_recv()
            w1_copy(d, p, source, 1 - m).wait_recv()

    for d in range(1, PLANE):
        w1_copy(d, (p + d) % PLANE, p, m).wait_send()

    def line_copy(b, way, to):
        ref = w_rows.at[:, pl.ds(b * PLANE * w_part, PLANE * w_part)]
        return remote(ref, ref, w2_send.at[b, way], w2_recv.at[b], to * PLANE + p, m)

    def line_round(step):
        for b in range(half_layers):
            distance = z - (m * half_layers + b)
            if step:
                @pl.when(jnp.logical_or(distance == step, distance == -step))
                def _():
                    line_copy(b, 0, z).wait_recv()

            @pl.when(jnp.logical_and(distance == step, z < layers - 1))
            def _():
                line_copy(b, 0, z + 1).start()

            @pl.when(jnp.logical_and(distance == -step, z > 0))
            def _():
                line_copy(b, 1, z - 1).start()

    def line_end():
        for b in range(half_layers):
            distance = z - (m * half_layers + b)

            @pl.when(jnp.logical_and(distance >= 0, z < layers - 1))
            def _():
                line_copy(b, 0, z).wait_send()

            @pl.when(jnp.logical_and(distance <= 0, z > 0))
            def _():
                line_copy(b, 1, z).wait_send()

    line_round(0)
    def far_head(t, carry):
        q, k, v = (moved[:, :, aligned(3 * t + i, depth)].reshape(rows, depth) for i in range(3))
        mixed = attend(q, k, v, t, (row_ids % group) // part, (col_ids % group) // part)
        result[:, :, aligned(t, depth)] = mixed.reshape(frames, group, depth)
        return carry

    def res_copy(c, d, to, slot):
        first, last = chunks[c]
        lanes = pl.ds(first * depth, (last - first) * depth)
        return remote(
            result.at[to, :, lanes], returned.at[slot, :, lanes],
            res_send.at[c, d], res_recv.at[c, d], to, m,
        )

    for c, (first, last) in enumerate(chunks):
        for d in range(1, frames):
            qkv_copy(c, d, me, (me + frames - d) % frames).wait_recv()
        lax.fori_loop(first, last, far_head, 0)
        for d in range(1, frames):
            res_copy(c, d, (me + d) % frames, me).start()
    returned[me] = result[me]
    line_round(1)

    def unpack(t, carry):
        at = aligned(t, depth)
        rows_back = jnp.dot(back, returned[:, :, at].reshape(rows, depth), preferred_element_type=f32)
        temporal = kinds_ref[:, at] == 1
        attended[p, :, at] = jnp.where(temporal, rows_back, attended[p, :, at].astype(f32)).astype(bf16)
        return carry

    for c, (first, last) in enumerate(chunks):
        for d in range(1, frames):
            res_copy(c, d, me, (me + frames - d) % frames).wait_recv()
        lax.fori_loop(first, last, unpack, 0)
        for d in range(1, PLANE):
            far_copy(c, d, (p + d) % PLANE, p).start()
        if c == len(chunks) - 2:
            line_round(2)
    for step in range(2 if len(chunks) < 2 else 3, layers):
        line_round(step)
    line_end()

    def order_rows(t, carry):
        h = head_of(t)
        for half in range(2):
            for i in range(pieces):
                w_slots[half, aligned(t * pieces + i, unit), :] = w_rows[half, h * pieces + i]
        return carry

    lax.fori_loop(0, heads, order_rows, 0)

    def part_copy(d):
        return remote(part_out.at[d], part_in.at[d], p_send.at[d], p_recv.at[d], me, 1 - m)

    for d in range(PLANE):
        source = (p + PLANE - d) % PLANE
        if d:
            if slots < heads:
                near_copy(d, p, source).wait_recv()
            for c in range(len(chunks)):
                far_copy(c, d, p, source).wait_recv()
        rows_in = attended[source]
        part_out[d] = jnp.dot(rows_in, w_slots[1 - m], preferred_element_type=f32)
        part_copy(d).start()
        part_own[d] = jnp.dot(rows_in, w_slots[m], preferred_element_type=f32)

    gate = gate_ref[:, aligned(p, columns)]

    def done_copy(d, to, source):
        return remote(
            done_out.at[d], done.at[:, aligned(source, columns)],
            o_send.at[d], o_recv.at[d], z * PLANE + to, m,
        )

    for d in range(PLANE):
        part_copy(d).wait_recv()
        gated = (gate * (part_own[d] + part_in[d])).astype(bf16)
        if d:
            done_out[d] = gated
            done_copy(d, (p + PLANE - d) % PLANE, p).start()
        else:
            done[:, aligned(p, columns)] = gated
    for d in range(1, frames):
        for c in range(len(chunks)):
            qkv_copy(c, d, (me + d) % frames, me).wait_send()
            res_copy(c, d, (me + d) % frames, me).wait_send()
    for d in range(PLANE):
        part_copy(d).wait_send()
    for d in range(1, PLANE):
        if slots < heads:
            near_copy(d, (p + d) % PLANE, p).wait_send()
        for c in range(len(chunks)):
            far_copy(c, d, (p + d) % PLANE, p).wait_send()
        done_copy(d, (p + PLANE - d) % PLANE, p).wait_send()
        done_copy(d, p, (p + d) % PLANE).wait_recv()
    out_ref[...] = done[...]


def branch_call(frames, slots, head_order, slot_kinds, slot_bias, order_map, q, k, v, w, gate):
    rows, width = q.shape
    heads = slot_bias.shape[0]
    depth = width // heads
    group, columns = rows // frames, width // PLANE
    half = w.shape[0] * frames // 2
    parts = len(slot_chunks(slots))
    unit = math.gcd(w.shape[0], depth)
    half_layers = frames // PLANE // 2
    bf16, f32, dma = jnp.bfloat16, jnp.float32, pltpu.SemaphoreType.DMA
    smem, vmem = pl.BlockSpec(memory_space=pltpu.SMEM), pl.BlockSpec(memory_space=pltpu.VMEM)
    return pl.pallas_call(
        functools.partial(branch_kernel, frames, slots, depth),
        out_shape=jax.ShapeDtypeStruct((rows, width), bf16),
        in_specs=[smem] + [pl.BlockSpec(memory_space=pl.ANY)] * 8,
        out_specs=vmem,
        scratch_shapes=[
            pltpu.VMEM(slot_kinds.shape, jnp.int32),
            pltpu.VMEM(slot_bias.shape, f32),
            pltpu.VMEM((1, rows), jnp.int32),
            pltpu.VMEM((heads, rows, depth), bf16),
            pltpu.VMEM((heads, rows, depth), bf16),
            pltpu.VMEM((heads, rows, depth), bf16),
            pltpu.VMEM((1, width), f32),
            dma((4,)),
            dma((3, heads)),
            pltpu.VMEM((frames, group, 3 * slots * depth), bf16),
            pltpu.VMEM((frames, group, 3 * slots * depth), bf16),
            pltpu.VMEM((frames, group, slots * depth), bf16),
            pltpu.VMEM((frames, group, slots * depth), bf16),
            pltpu.VMEM((PLANE, rows, width), bf16),
            pltpu.VMEM((2, half // unit, unit, columns), bf16),
            pltpu.VMEM((2, half, columns), bf16),
            pltpu.VMEM((PLANE, rows, columns), f32),
            pltpu.VMEM((PLANE, rows, columns), f32),
            pltpu.VMEM((PLANE, rows, columns), f32),
            pltpu.VMEM((PLANE, rows, columns), bf16),
            pltpu.VMEM((rows, width), bf16),
            dma((parts, frames)), dma((parts, frames)), dma((parts, frames)), dma((parts, frames)),
            dma((PLANE,)), dma((PLANE,)), dma((parts, PLANE)), dma((parts, PLANE)),
            dma((PLANE,)), dma((PLANE, 2)), dma(()), dma((half_layers, 2)), dma((half_layers,)),
            dma((PLANE,)), dma((PLANE,)), dma((PLANE,)), dma((PLANE,)),
        ],
        compiler_params=pltpu.CompilerParams(
            collective_id=slots, has_side_effects=True, vmem_limit_bytes=48 * 2**20
        ),
        name="branch_%d" % slots,
    )(
        head_order, slot_kinds, slot_bias, order_map.reshape(1, rows),
        q, k, v, w.reshape(-1, unit, width), gate.reshape(1, width),
    )


def count_kernel(sizes, kinds_ref, row_ref, branch_ref, order_ref, mine, other, send, recv):
    me, m = lax.axis_index("seq"), lax.axis_index("mlp")
    heads = kinds_ref.shape[0]
    barrier = pltpu.get_barrier_semaphore()
    pl.semaphore_signal(barrier, inc=1, device_id=(me, 1 - m), device_id_type=MESH)
    mine[...] = jnp.zeros_like(mine)
    mine[0:1, 0:heads] = row_ref[...]
    pl.semaphore_wait(barrier, 1)
    copy = pltpu.make_async_remote_copy(
        src_ref=mine, dst_ref=other, send_sem=send, recv_sem=recv,
        device_id=(me, 1 - m), device_id_type=MESH,
    )
    copy.start()
    kinds = [kinds_ref[h] for h in range(heads)]
    far, near, slots = 0, sum(kinds), []
    for kind in kinds:
        slots.append(kind * far + (1 - kind) * near)
        far, near = far + kind, near + 1 - kind
    for t in range(heads):
        order_ref[t] = sum(h * (slots[h] == t).astype(jnp.int32) for h in range(heads))
    copy.wait()
    most = jnp.maximum(jnp.sum(mine[...]), jnp.sum(other[...]))
    branch_ref[0] = sum((most > size).astype(jnp.int32) for size in sizes)


def choose(sizes, head_kinds):
    heads = head_kinds.shape[0]
    smem, dma = pl.BlockSpec(memory_space=pltpu.SMEM), pltpu.SemaphoreType.DMA
    return pl.pallas_call(
        functools.partial(count_kernel, sizes),
        out_shape=[jax.ShapeDtypeStruct((1,), jnp.int32), jax.ShapeDtypeStruct((heads,), jnp.int32)],
        in_specs=[smem, pl.BlockSpec(memory_space=pltpu.VMEM)],
        out_specs=[smem, smem],
        scratch_shapes=[pltpu.VMEM((8, 128), jnp.int32)] * 2 + [dma(()), dma(())],
        compiler_params=pltpu.CompilerParams(collective_id=64, has_side_effects=True),
        name="count_temporal",
    )(head_kinds, head_kinds[None, :])


def fused_local(q, k, v, head_kinds, block_masks, order_map, out_weight, gate_values):
    frames = lax.axis_size("seq")
    heads = head_kinds.shape[0]
    depth = q.shape[1] // heads
    sizes = list(range(heads // 3, heads))
    branch, order = choose(sizes, head_kinds)
    ids = jnp.arange(heads, dtype=jnp.int32)
    bias = jnp.where(block_masks == 1, 0.0, -1e30).reshape(heads, 4)
    spread = lambda kinds: jnp.repeat(kinds, depth)[None, :]
    widen = lambda levels: jnp.broadcast_to(levels[:, :, None], (heads, 4, depth))

    def by_slot(slots):
        chosen = order[:, None] == ids[None, :]
        kinds = jnp.sum(jnp.where(chosen, head_kinds[None, :], 0), axis=1)
        levels = jnp.sum(jnp.where(chosen[:, :, None], bias[None, :, :], 0.0), axis=1)
        return call(slots, order, kinds, levels)

    def call(slots, order, kinds, bias):
        return branch_call(
            frames, slots, order, spread(kinds), widen(bias),
            order_map, q, k, v, out_weight, gate_values,
        )

    branches = [functools.partial(by_slot, size) for size in sizes]
    branches.append(functools.partial(call, heads, ids, head_kinds, bias))
    return lax.switch(branch[0], branches)


def fits(mesh):
    frames = mesh.shape["seq"]
    return mesh.shape["mlp"] == 2 and frames % (2 * PLANE) == 0 and frames <= 16


def solution(mesh):
    in_specs = (
        P("seq", "mlp"),
        P("seq", "mlp"),
        P("seq", "mlp"),
        P("mlp"),
        P("mlp", None, None),
        P(),
        P("seq", "mlp"),
        P("mlp"),
    )
    out_specs = P("seq", "mlp")
    body = fused_local if fits(mesh) else local
    return jax.shard_map(body, mesh=mesh, in_specs=in_specs, out_specs=out_specs, check_vma=False)
```

```python
import functools
import math

import jax
import jax.numpy as jnp
from jax import lax
from jax.experimental import pallas as pl
from jax.experimental.pallas import tpu as pltpu
from jax.sharding import PartitionSpec as P


def attend_rows(query_rows, key_rows, value_rows, visible):
    row_count, head_count, head_depth = query_rows.shape
    score_scale = 1.0 / math.sqrt(head_depth)
    scores = (
        jnp.einsum("qhd,khd->hqk", query_rows, key_rows, preferred_element_type=jnp.float32)
        * score_scale
    )
    row_max = jnp.max(jnp.where(visible, scores, -jnp.inf), axis=2, keepdims=True)
    weights = jnp.where(visible, jnp.exp(scores - row_max), 0.0)
    row_total = jnp.sum(weights, axis=2)
    combined = jnp.einsum(
        "hqk,khd->qhd", weights.astype(jnp.bfloat16), value_rows, preferred_element_type=jnp.float32
    )
    outputs = (combined / jnp.transpose(row_total)[:, :, None]).astype(jnp.bfloat16)
    return outputs


def to_positions(query_rows, key_rows, value_rows, frames, group_size):
    row_width = query_rows.shape[1]
    exchanged = (
        lax.all_to_all(
            query_rows.reshape(frames, group_size, 1, row_width),
            "seq",
            split_axis=0,
            concat_axis=2,
            tiled=True,
        ),
        lax.all_to_all(
            key_rows.reshape(frames, group_size, 1, row_width),
            "seq",
            split_axis=0,
            concat_axis=2,
            tiled=True,
        ),
        lax.all_to_all(
            value_rows.reshape(frames, group_size, 1, row_width),
            "seq",
            split_axis=0,
            concat_axis=2,
            tiled=True,
        ),
    )
    return tuple((member.reshape(group_size * frames, row_width) for member in exchanged))


def to_frames(results, frames, group_size):
    row_width = results.shape[1]
    exchanged = lax.all_to_all(
        results.reshape(1, group_size, frames, row_width),
        "seq",
        split_axis=2,
        concat_axis=0,
        tiled=True,
    )
    return exchanged.reshape(frames * group_size, row_width)


def split_heads(array, head_count):
    return array.reshape(array.shape[0], head_count, array.shape[1] // head_count)


def local(
    queries, key_vectors, value_vectors, head_kinds, block_masks, order_map, out_weight, gate_values
):
    row_count, row_width = queries.shape
    head_count = head_kinds.shape[0]
    frames = lax.axis_size("seq")
    group_size = row_count // frames
    block_size = row_count // block_masks.shape[1]
    inverse = (
        jnp.zeros((row_count,), jnp.int32).at[order_map].set(jnp.arange(row_count, dtype=jnp.int32))
    )
    visible = jnp.repeat(jnp.repeat(block_masks == 1, block_size, axis=1), block_size, axis=2)
    temporal = (head_kinds == 1)[None, :, None]
    moved_queries, moved_keys, moved_values = to_positions(
        queries[order_map], key_vectors[order_map], value_vectors[order_map], frames, group_size
    )
    near_result = attend_rows(
        split_heads(queries, head_count),
        split_heads(key_vectors, head_count),
        split_heads(value_vectors, head_count),
        visible,
    )
    far_result = attend_rows(
        split_heads(moved_queries, head_count),
        split_heads(moved_keys, head_count),
        split_heads(moved_values, head_count),
        visible,
    )
    returned = to_frames(far_result.reshape(row_count, row_width), frames, group_size)[inverse]
    per_head = jnp.where(temporal, split_heads(returned, head_count), near_result)
    attended = per_head.reshape(row_count, row_width)
    head_columns = lax.all_gather(attended, "mlp", axis=1, tiled=True)
    projected = jnp.dot(
        head_columns,
        lax.all_gather(out_weight, "seq", axis=0, tiled=True),
        preferred_element_type=jnp.float32,
    )
    return (gate_values[None, :] * projected).astype(jnp.bfloat16)


PLANE = 4
MESH = pl.DeviceIdType.MESH


def aligned(index, size):
    return pl.ds(pl.multiple_of(index * size, size), size)


def each(first, last):
    def run(body):
        def step(i, carry):
            body(i)
            return carry

        lax.fori_loop(first, last, step, 0)

    return run


def slot_chunks(slots):
    parts = max(1, min(4, slots // 2))
    edges = [slots * i // parts for i in range(parts + 1)]
    return list(zip(edges[:-1], edges[1:]))


def branch_kernel(
    frames, slots, depth,
    heads_ref, kinds_hbm, bias_hbm, order_hbm, q_hbm, k_hbm, v_hbm, w_ref, gate_hbm,
    out_ref,
    kinds_ref, bias_ref, order_ref, q_ref, k_ref, v_ref, gate_ref, fetch_sem, head_sem,
    packed, moved, result, returned, attended, w_rows, w_slots, part_out, part_own, part_in,
    done_out, done,
    qkv_send, qkv_recv, res_send, res_recv, near_send, near_recv, far_send, far_recv,
    w1_send, w1_recv, w1_own, w2_send, w2_recv, p_send, p_recv, o_send, o_recv,
):
    rows, width = q_hbm.shape
    heads = width // depth
    group = rows // frames
    layers = frames // PLANE
    half_layers = layers // 2
    w_part, unit = w_ref.shape[:2]
    pieces, columns = depth // unit, width // PLANE
    me, m = lax.axis_index("seq"), lax.axis_index("mlp")
    z, p = me // PLANE, me % PLANE
    scale = 1.0 / math.sqrt(depth)
    bf16, f32 = jnp.bfloat16, jnp.float32

    def remote(src, dst, send, recv, seq, mlp):
        return pltpu.make_async_remote_copy(
            src_ref=src, dst_ref=dst, send_sem=send, recv_sem=recv,
            device_id=(seq, mlp), device_id_type=MESH,
        )

    fetches = [
        pltpu.make_async_copy(src, dst, fetch_sem.at[i])
        for i, (src, dst) in enumerate((
            (order_hbm, order_ref), (bias_hbm, bias_ref), (kinds_hbm, kinds_ref), (gate_hbm, gate_ref),
        ))
    ]

    def head_fetches(h):
        return [
            pltpu.make_async_copy(src.at[:, aligned(h, depth)], dst.at[h], head_sem.at[i, h])
            for i, (src, dst) in enumerate(((q_hbm, q_ref), (k_hbm, k_ref), (v_hbm, v_ref)))
        ]

    for fetch in fetches:
        fetch.start()

    @each(0, heads)
    def _(h):
        for fetch in head_fetches(h):
            fetch.start()

    barrier = pltpu.get_barrier_semaphore()
    pl.semaphore_signal(barrier, inc=1, device_id=(me, 1 - m), device_id_type=MESH)

    @each(1, frames)
    def _(d):
        peer = (me + d) % frames
        pl.semaphore_signal(barrier, inc=1, device_id=(peer, m), device_id_type=MESH)
        pl.semaphore_signal(barrier, inc=1, device_id=(peer, 1 - m), device_id_type=MESH)

    for fetch in fetches:
        fetch.wait()

    @each(0, heads)
    def _(h):
        for fetch in head_fetches(h):
            fetch.wait()

    places = lax.broadcasted_iota(jnp.int32, (rows, rows), 0)
    back_f32 = jnp.where(places == order_ref[...], 1.0, 0.0)
    back = back_f32.astype(bf16)
    forth = back_f32.T.astype(bf16)

    def head_of(t):
        return t if slots == heads else heads_ref[t]

    def pack(t, carry):
        h = head_of(t)
        for i, ref in enumerate((q_ref, k_ref, v_ref)):
            block = jnp.dot(forth, ref[h], preferred_element_type=f32)
            packed[:, :, aligned(3 * t + i, depth)] = block.astype(bf16).reshape(frames, group, depth)
        return carry

    chunks = slot_chunks(slots)

    def qkv_copy(c, d, to, slot):
        first, last = chunks[c]
        lanes = pl.ds(3 * first * depth, 3 * (last - first) * depth)
        return remote(
            packed.at[to, :, lanes], moved.at[slot, :, lanes],
            qkv_send.at[c, d], qkv_recv.at[c, d], to, m,
        )

    for c, (first, last) in enumerate(chunks):
        lax.fori_loop(first, last, pack, 0)
        if c == 0:
            pl.semaphore_wait(barrier, 2 * frames - 1)

        @each(1, frames)
        def _(d):
            qkv_copy(c, d, (me + d) % frames, me).start()

    moved[me] = packed[me]

    core = z // half_layers
    layer = z % half_layers

    def w1_copy(d, to, source, source_m):
        return remote(
            w_ref.at[:, :, aligned(to, columns)],
            w_rows.at[source_m, aligned(layer * PLANE + source, w_part)],
            w1_send.at[d], w1_recv.at[d, source_m], z * PLANE + to, core,
        )

    for d in range(1, PLANE):
        w1_copy(d, (p + d) % PLANE, p, m).start()

    @pl.when(m != core)
    def _():
        w1_copy(0, p, p, m).start()

    own_copy = pltpu.make_async_copy(
        w_ref.at[:, :, aligned(p, columns)],
        w_rows.at[m, aligned(layer * PLANE + p, w_part)],
        w1_own,
    )

    @pl.when(m == core)
    def _():
        own_copy.start()

    row_ids = lax.broadcasted_iota(jnp.int32, (rows, rows), 0)
    col_ids = lax.broadcasted_iota(jnp.int32, (rows, rows), 1)
    block = rows // 2
    part = block // frames
    assert 2 * block == rows and 2 * part == group

    def attend(q, k, v, t, row_block, col_block):
        levels = bias_ref[t]
        levels = jnp.concatenate([levels, levels], axis=1)
        first = col_block[0:1] == 0
        upper = jnp.where(first, levels[0:1], levels[1:2])
        lower = jnp.where(first, levels[2:3], levels[3:4])
        bias = jnp.where(row_block == 0, upper, lower)
        scores = lax.dot_general(q, k, (((1,), (1,)), ((), ())), preferred_element_type=f32)
        scores = scores * scale + bias
        weights = jnp.exp(scores - jnp.max(scores, axis=1, keepdims=True))
        total = jnp.sum(weights, axis=1, keepdims=True)
        mixed = jnp.dot(weights.astype(bf16), v, preferred_element_type=f32)
        return (mixed / total).astype(bf16)

    def attend_slots(first, last, load, blocks, store):
        def step(start, count):
            loaded = [load(start + i) for i in range(count)]
            mixed = [attend(*loaded[i], start + i, *blocks) for i in range(count)]
            for i in range(count):
                store(start + i, mixed[i])

        @each(0, (last - first) // 2)
        def _(pair):
            step(first + 2 * pair, 2)

        if (last - first) % 2:
            step(last - 1, 1)

    near_blocks = (row_ids // block, col_ids // block)
    far_blocks = ((row_ids % group) // part, (col_ids % group) // part)

    def near_load(t):
        h = head_of(t)
        return q_ref[h], k_ref[h], v_ref[h]

    def near_store(t, mixed):
        attended[p, :, aligned(t, depth)] = mixed

    def far_load(t):
        return [moved[:, :, aligned(3 * t + i, depth)].reshape(rows, depth) for i in range(3)]

    def far_store(t, mixed):
        result[:, :, aligned(t, depth)] = mixed.reshape(frames, group, depth)

    near_cols = pl.ds(slots * depth, (heads - slots) * depth)

    def near_copy(d, to, source):
        ref = attended.at[source, :, near_cols]
        return remote(ref, ref, near_send.at[d], near_recv.at[d], z * PLANE + to, m)

    def far_copy(c, d, to, source):
        first, last = chunks[c]
        ref = attended.at[source, :, pl.ds(first * depth, (last - first) * depth)]
        return remote(ref, ref, far_send.at[c, d], far_recv.at[c, d], z * PLANE + to, m)

    if slots < heads:
        attend_slots(slots, heads, near_load, near_blocks, near_store)
        for d in range(1, PLANE):
            near_copy(d, (p + d) % PLANE, p).start()

    @pl.when(m != core)
    def _():
        w1_copy(0, p, p, m).wait_send()

    @pl.when(m == core)
    def _():
        own_copy.wait()
        for d in range(PLANE):
            source = (p + PLANE - d) % PLANE
            if d:
                w1_copy(d, p, source, m).wait_recv()
            w1_copy(d, p, source, 1 - m).wait_recv()

    for d in range(1, PLANE):
        w1_copy(d, (p + d) % PLANE, p, m).wait_send()

    def line_copy(b, way, to):
        ref = w_rows.at[:, pl.ds(b * PLANE * w_part, PLANE * w_part)]
        return remote(ref, ref, w2_send.at[b, way], w2_recv.at[b], to * PLANE + p, m)

    def line_round(step):
        for b in range(half_layers):
            distance = z - (m * half_layers + b)
            if step:
                @pl.when(jnp.logical_or(distance == step, distance == -step))
                def _():
                    line_copy(b, 0, z).wait_recv()

            @pl.when(jnp.logical_and(distance == step, z < layers - 1))
            def _():
                line_copy(b, 0, z + 1).start()

            @pl.when(jnp.logical_and(distance == -step, z > 0))
            def _():
                line_copy(b, 1, z - 1).start()

    def line_end():
        for b in range(half_layers):
            distance = z - (m * half_layers + b)

            @pl.when(jnp.logical_and(distance >= 0, z < layers - 1))
            def _():
                line_copy(b, 0, z).wait_send()

            @pl.when(jnp.logical_and(distance <= 0, z > 0))
            def _():
                line_copy(b, 1, z).wait_send()

    line_round(0)
    def res_copy(c, d, to, slot):
        first, last = chunks[c]
        lanes = pl.ds(first * depth, (last - first) * depth)
        return remote(
            result.at[to, :, lanes], returned.at[slot, :, lanes],
            res_send.at[c, d], res_recv.at[c, d], to, m,
        )

    for c, (first, last) in enumerate(chunks):
        @each(1, frames)
        def _(d):
            qkv_copy(c, d, me, (me + frames - d) % frames).wait_recv()

        attend_slots(first, last, far_load, far_blocks, far_store)

        @each(1, frames)
        def _(d):
            res_copy(c, d, (me + d) % frames, me).start()

    returned[me] = result[me]
    line_round(1)
    attend_slots(0, slots, near_load, near_blocks, near_store)

    def unpack(t, carry):
        at = aligned(t, depth)
        rows_back = jnp.dot(back, returned[:, :, at].reshape(rows, depth), preferred_element_type=f32)
        temporal = kinds_ref[:, at] == 1
        attended[p, :, at] = jnp.where(temporal, rows_back, attended[p, :, at].astype(f32)).astype(bf16)
        return carry

    for c, (first, last) in enumerate(chunks):
        @each(1, frames)
        def _(d):
            res_copy(c, d, me, (me + frames - d) % frames).wait_recv()

        lax.fori_loop(first, last, unpack, 0)
        for d in range(1, PLANE):
            far_copy(c, d, (p + d) % PLANE, p).start()
        if c == len(chunks) - 2:
            line_round(2)
    for step in range(2 if len(chunks) < 2 else 3, layers):
        line_round(step)
    line_end()

    def order_rows(t, carry):
        h = head_of(t)
        for half in range(2):
            for i in range(pieces):
                w_slots[half, aligned(t * pieces + i, unit), :] = w_rows[half, h * pieces + i]
        return carry

    lax.fori_loop(0, heads, order_rows, 0)

    def part_copy(d):
        return remote(part_out.at[d], part_in.at[d], p_send.at[d], p_recv.at[d], me, 1 - m)

    @each(0, PLANE)
    def _(d):
        source = (p + PLANE - d) % PLANE

        @pl.when(d > 0)
        def _():
            if slots < heads:
                near_copy(d, p, source).wait_recv()
            for c in range(len(chunks)):
                far_copy(c, d, p, source).wait_recv()

        rows_in = attended[source]
        part_out[d] = jnp.dot(rows_in, w_slots[1 - m], preferred_element_type=f32)
        part_copy(d).start()
        part_own[d] = jnp.dot(rows_in, w_slots[m], preferred_element_type=f32)

    gate = gate_ref[:, aligned(p, columns)]

    def done_copy(d, to, source):
        return remote(
            done_out.at[d], done.at[:, aligned(source, columns)],
            o_send.at[d], o_recv.at[d], z * PLANE + to, m,
        )

    def gated(d):
        part_copy(d).wait_recv()
        return (gate * (part_own[d] + part_in[d])).astype(bf16)

    done[:, aligned(p, columns)] = gated(0)

    @each(1, PLANE)
    def _(d):
        done_out[d] = gated(d)
        done_copy(d, (p + PLANE - d) % PLANE, p).start()

    @each(1, frames)
    def _(d):
        for c in range(len(chunks)):
            qkv_copy(c, d, (me + d) % frames, me).wait_send()
            res_copy(c, d, (me + d) % frames, me).wait_send()

    part_copy(0).wait_send()

    @each(1, PLANE)
    def _(d):
        part_copy(d).wait_send()
        if slots < heads:
            near_copy(d, (p + d) % PLANE, p).wait_send()
        for c in range(len(chunks)):
            far_copy(c, d, (p + d) % PLANE, p).wait_send()
        done_copy(d, (p + PLANE - d) % PLANE, p).wait_send()
        done_copy(d, p, (p + d) % PLANE).wait_recv()

    out_ref[...] = done[...]


def branch_call(frames, slots, head_order, slot_kinds, slot_bias, order_map, q, k, v, w, gate):
    rows, width = q.shape
    heads = slot_bias.shape[0]
    depth = width // heads
    group, columns = rows // frames, width // PLANE
    half = w.shape[0] * frames // 2
    parts = len(slot_chunks(slots))
    unit = math.gcd(w.shape[0], depth)
    half_layers = frames // PLANE // 2
    bf16, f32, dma = jnp.bfloat16, jnp.float32, pltpu.SemaphoreType.DMA
    smem, vmem = pl.BlockSpec(memory_space=pltpu.SMEM), pl.BlockSpec(memory_space=pltpu.VMEM)
    return pl.pallas_call(
        functools.partial(branch_kernel, frames, slots, depth),
        out_shape=jax.ShapeDtypeStruct((rows, width), bf16),
        in_specs=[smem] + [pl.BlockSpec(memory_space=pl.ANY)] * 8,
        out_specs=vmem,
        scratch_shapes=[
            pltpu.VMEM(slot_kinds.shape, jnp.int32),
            pltpu.VMEM(slot_bias.shape, f32),
            pltpu.VMEM((1, rows), jnp.int32),
            pltpu.VMEM((heads, rows, depth), bf16),
            pltpu.VMEM((heads, rows, depth), bf16),
            pltpu.VMEM((heads, rows, depth), bf16),
            pltpu.VMEM((1, width), f32),
            dma((4,)),
            dma((3, heads)),
            pltpu.VMEM((frames, group, 3 * slots * depth), bf16),
            pltpu.VMEM((frames, group, 3 * slots * depth), bf16),
            pltpu.VMEM((frames, group, slots * depth), bf16),
            pltpu.VMEM((frames, group, slots * depth), bf16),
            pltpu.VMEM((PLANE, rows, width), bf16),
            pltpu.VMEM((2, half // unit, unit, columns), bf16),
            pltpu.VMEM((2, half, columns), bf16),
            pltpu.VMEM((PLANE, rows, columns), f32),
            pltpu.VMEM((PLANE, rows, columns), f32),
            pltpu.VMEM((PLANE, rows, columns), f32),
            pltpu.VMEM((PLANE, rows, columns), bf16),
            pltpu.VMEM((rows, width), bf16),
            dma((parts, frames)), dma((parts, frames)), dma((parts, frames)), dma((parts, frames)),
            dma((PLANE,)), dma((PLANE,)), dma((parts, PLANE)), dma((parts, PLANE)),
            dma((PLANE,)), dma((PLANE, 2)), dma(()), dma((half_layers, 2)), dma((half_layers,)),
            dma((PLANE,)), dma((PLANE,)), dma((PLANE,)), dma((PLANE,)),
        ],
        compiler_params=pltpu.CompilerParams(
            collective_id=slots, has_side_effects=True, vmem_limit_bytes=48 * 2**20
        ),
        name="branch_%d" % slots,
    )(
        head_order, slot_kinds, slot_bias, order_map.reshape(1, rows),
        q, k, v, w.reshape(-1, unit, width), gate.reshape(1, width),
    )


def count_kernel(sizes, kinds_ref, row_ref, branch_ref, order_ref, mine, other, send, recv):
    me, m = lax.axis_index("seq"), lax.axis_index("mlp")
    heads = kinds_ref.shape[0]
    barrier = pltpu.get_barrier_semaphore()
    pl.semaphore_signal(barrier, inc=1, device_id=(me, 1 - m), device_id_type=MESH)
    mine[...] = jnp.zeros_like(mine)
    mine[0:1, 0:heads] = row_ref[...]
    pl.semaphore_wait(barrier, 1)
    copy = pltpu.make_async_remote_copy(
        src_ref=mine, dst_ref=other, send_sem=send, recv_sem=recv,
        device_id=(me, 1 - m), device_id_type=MESH,
    )
    copy.start()
    kinds = [kinds_ref[h] for h in range(heads)]
    far, near, slots = 0, sum(kinds), []
    for kind in kinds:
        slots.append(kind * far + (1 - kind) * near)
        far, near = far + kind, near + 1 - kind
    for t in range(heads):
        order_ref[t] = sum(h * (slots[h] == t).astype(jnp.int32) for h in range(heads))
    copy.wait()
    most = jnp.maximum(jnp.sum(mine[...]), jnp.sum(other[...]))
    branch_ref[0] = sum((most > size).astype(jnp.int32) for size in sizes)


def choose(sizes, head_kinds):
    heads = head_kinds.shape[0]
    smem, dma = pl.BlockSpec(memory_space=pltpu.SMEM), pltpu.SemaphoreType.DMA
    return pl.pallas_call(
        functools.partial(count_kernel, sizes),
        out_shape=[jax.ShapeDtypeStruct((1,), jnp.int32), jax.ShapeDtypeStruct((heads,), jnp.int32)],
        in_specs=[smem, pl.BlockSpec(memory_space=pltpu.VMEM)],
        out_specs=[smem, smem],
        scratch_shapes=[pltpu.VMEM((8, 128), jnp.int32)] * 2 + [dma(()), dma(())],
        compiler_params=pltpu.CompilerParams(collective_id=64, has_side_effects=True),
        name="count_temporal",
    )(head_kinds, head_kinds[None, :])


def fused_local(q, k, v, head_kinds, block_masks, order_map, out_weight, gate_values):
    frames = lax.axis_size("seq")
    heads = head_kinds.shape[0]
    depth = q.shape[1] // heads
    sizes = list(range(heads // 2 - 1, heads // 2 + 4))
    branch, order = choose(sizes, head_kinds)
    ids = jnp.arange(heads, dtype=jnp.int32)
    bias = jnp.where(block_masks == 1, 0.0, -1e30).reshape(heads, 4)
    spread = lambda kinds: jnp.repeat(kinds, depth)[None, :]
    widen = lambda levels: jnp.broadcast_to(levels[:, :, None], (heads, 4, depth))

    def by_slot(slots):
        chosen = order[:, None] == ids[None, :]
        kinds = jnp.sum(jnp.where(chosen, head_kinds[None, :], 0), axis=1)
        levels = jnp.sum(jnp.where(chosen[:, :, None], bias[None, :, :], 0.0), axis=1)
        return call(slots, order, kinds, levels)

    def call(slots, order, kinds, bias):
        return branch_call(
            frames, slots, order, spread(kinds), widen(bias),
            order_map, q, k, v, out_weight, gate_values,
        )

    branches = [functools.partial(by_slot, size) for size in sizes]
    branches.append(functools.partial(call, heads, ids, head_kinds, bias))
    return lax.switch(branch[0], branches)


def fits(mesh):
    frames = mesh.shape["seq"]
    return mesh.shape["mlp"] == 2 and frames % (2 * PLANE) == 0 and frames <= 16


def solution(mesh):
    in_specs = (
        P("seq", "mlp"),
        P("seq", "mlp"),
        P("seq", "mlp"),
        P("mlp"),
        P("mlp", None, None),
        P(),
        P("seq", "mlp"),
        P("mlp"),
    )
    out_specs = P("seq", "mlp")
    body = fused_local if fits(mesh) else local
    return jax.shard_map(body, mesh=mesh, in_specs=in_specs, out_specs=out_specs, check_vma=False)
```

```python
import functools
import math

import jax
import jax.numpy as jnp
from jax import lax
from jax.experimental import pallas as pl
from jax.experimental.pallas import tpu as pltpu
from jax.sharding import PartitionSpec as P


def attend_rows(query_rows, key_rows, value_rows, visible):
    row_count, head_count, head_depth = query_rows.shape
    score_scale = 1.0 / math.sqrt(head_depth)
    scores = (
        jnp.einsum("qhd,khd->hqk", query_rows, key_rows, preferred_element_type=jnp.float32)
        * score_scale
    )
    row_max = jnp.max(jnp.where(visible, scores, -jnp.inf), axis=2, keepdims=True)
    weights = jnp.where(visible, jnp.exp(scores - row_max), 0.0)
    row_total = jnp.sum(weights, axis=2)
    combined = jnp.einsum(
        "hqk,khd->qhd", weights.astype(jnp.bfloat16), value_rows, preferred_element_type=jnp.float32
    )
    outputs = (combined / jnp.transpose(row_total)[:, :, None]).astype(jnp.bfloat16)
    return outputs


def to_positions(query_rows, key_rows, value_rows, frames, group_size):
    row_width = query_rows.shape[1]
    exchanged = (
        lax.all_to_all(
            query_rows.reshape(frames, group_size, 1, row_width),
            "seq",
            split_axis=0,
            concat_axis=2,
            tiled=True,
        ),
        lax.all_to_all(
            key_rows.reshape(frames, group_size, 1, row_width),
            "seq",
            split_axis=0,
            concat_axis=2,
            tiled=True,
        ),
        lax.all_to_all(
            value_rows.reshape(frames, group_size, 1, row_width),
            "seq",
            split_axis=0,
            concat_axis=2,
            tiled=True,
        ),
    )
    return tuple((member.reshape(group_size * frames, row_width) for member in exchanged))


def to_frames(results, frames, group_size):
    row_width = results.shape[1]
    exchanged = lax.all_to_all(
        results.reshape(1, group_size, frames, row_width),
        "seq",
        split_axis=2,
        concat_axis=0,
        tiled=True,
    )
    return exchanged.reshape(frames * group_size, row_width)


def split_heads(array, head_count):
    return array.reshape(array.shape[0], head_count, array.shape[1] // head_count)


def local(
    queries, key_vectors, value_vectors, head_kinds, block_masks, order_map, out_weight, gate_values
):
    row_count, row_width = queries.shape
    head_count = head_kinds.shape[0]
    frames = lax.axis_size("seq")
    group_size = row_count // frames
    block_size = row_count // block_masks.shape[1]
    inverse = (
        jnp.zeros((row_count,), jnp.int32).at[order_map].set(jnp.arange(row_count, dtype=jnp.int32))
    )
    visible = jnp.repeat(jnp.repeat(block_masks == 1, block_size, axis=1), block_size, axis=2)
    temporal = (head_kinds == 1)[None, :, None]
    moved_queries, moved_keys, moved_values = to_positions(
        queries[order_map], key_vectors[order_map], value_vectors[order_map], frames, group_size
    )
    near_result = attend_rows(
        split_heads(queries, head_count),
        split_heads(key_vectors, head_count),
        split_heads(value_vectors, head_count),
        visible,
    )
    far_result = attend_rows(
        split_heads(moved_queries, head_count),
        split_heads(moved_keys, head_count),
        split_heads(moved_values, head_count),
        visible,
    )
    returned = to_frames(far_result.reshape(row_count, row_width), frames, group_size)[inverse]
    per_head = jnp.where(temporal, split_heads(returned, head_count), near_result)
    attended = per_head.reshape(row_count, row_width)
    head_columns = lax.all_gather(attended, "mlp", axis=1, tiled=True)
    projected = jnp.dot(
        head_columns,
        lax.all_gather(out_weight, "seq", axis=0, tiled=True),
        preferred_element_type=jnp.float32,
    )
    return (gate_values[None, :] * projected).astype(jnp.bfloat16)


PLANE = 4
MESH = pl.DeviceIdType.MESH


def aligned(index, size):
    return pl.ds(pl.multiple_of(index * size, size), size)


def each(first, last):
    def run(body):
        def step(i, carry):
            body(i)
            return carry

        lax.fori_loop(first, last, step, 0)

    return run


def slot_chunks(slots):
    parts = max(1, min(4, slots // 2))
    edges = [slots * i // parts for i in range(parts + 1)]
    return list(zip(edges[:-1], edges[1:]))


def branch_kernel(
    frames, slots, depth,
    heads_ref, kinds_hbm, bias_hbm, order_hbm, q_hbm, k_hbm, v_hbm, w_ref, gate_hbm,
    out_ref,
    kinds_ref, bias_ref, order_ref, q_ref, k_ref, v_ref, gate_ref, fetch_sem, head_sem,
    packed, moved, result, returned, attended, w_rows, w_slots, part_out, part_own, part_in,
    done_out, done,
    qkv_send, qkv_recv, res_send, res_recv, near_send, near_recv, far_send, far_recv,
    w1_send, w1_recv, w1_own, w2_send, w2_recv, p_send, p_recv, o_send, o_recv,
):
    rows, width = q_hbm.shape
    heads = width // depth
    group = rows // frames
    layers = frames // PLANE
    half_layers = layers // 2
    w_part, unit = w_ref.shape[:2]
    pieces, columns = depth // unit, width // PLANE
    me, m = lax.axis_index("seq"), lax.axis_index("mlp")
    z, p = me // PLANE, me % PLANE
    scale = 1.0 / math.sqrt(depth)
    bf16, f32 = jnp.bfloat16, jnp.float32

    def remote(src, dst, send, recv, seq, mlp):
        return pltpu.make_async_remote_copy(
            src_ref=src, dst_ref=dst, send_sem=send, recv_sem=recv,
            device_id=(seq, mlp), device_id_type=MESH,
        )

    fetches = [
        pltpu.make_async_copy(src, dst, fetch_sem.at[i])
        for i, (src, dst) in enumerate((
            (order_hbm, order_ref), (bias_hbm, bias_ref), (kinds_hbm, kinds_ref), (gate_hbm, gate_ref),
        ))
    ]

    def head_fetches(h):
        return [
            pltpu.make_async_copy(src.at[:, aligned(h, depth)], dst.at[h], head_sem.at[i, h])
            for i, (src, dst) in enumerate(((q_hbm, q_ref), (k_hbm, k_ref), (v_hbm, v_ref)))
        ]

    for fetch in fetches:
        fetch.start()

    @each(0, heads)
    def _(h):
        for fetch in head_fetches(h):
            fetch.start()

    barrier = pltpu.get_barrier_semaphore()
    pl.semaphore_signal(barrier, inc=1, device_id=(me, 1 - m), device_id_type=MESH)

    @each(1, frames)
    def _(d):
        peer = (me + d) % frames
        pl.semaphore_signal(barrier, inc=1, device_id=(peer, m), device_id_type=MESH)
        pl.semaphore_signal(barrier, inc=1, device_id=(peer, 1 - m), device_id_type=MESH)

    pl.semaphore_wait(barrier, 2 * frames - 1)

    core = z // half_layers
    layer = z % half_layers

    def w1_copy(d, to, source, source_m):
        return remote(
            w_ref.at[:, :, aligned(to, columns)],
            w_rows.at[source_m, aligned(layer * PLANE + source, w_part)],
            w1_send.at[d], w1_recv.at[d, source_m], z * PLANE + to, core,
        )

    for d in range(1, PLANE):
        w1_copy(d, (p + d) % PLANE, p, m).start()

    @pl.when(m != core)
    def _():
        w1_copy(0, p, p, m).start()

    own_copy = pltpu.make_async_copy(
        w_ref.at[:, :, aligned(p, columns)],
        w_rows.at[m, aligned(layer * PLANE + p, w_part)],
        w1_own,
    )

    @pl.when(m == core)
    def _():
        own_copy.start()

    for fetch in fetches:
        fetch.wait()

    @each(0, heads)
    def _(h):
        for fetch in head_fetches(h):
            fetch.wait()

    places = lax.broadcasted_iota(jnp.int32, (rows, rows), 0)
    back_f32 = jnp.where(places == order_ref[...], 1.0, 0.0)
    back = back_f32.astype(bf16)
    forth = back_f32.T.astype(bf16)

    def head_of(t):
        return t if slots == heads else heads_ref[t]

    def pack(t, carry):
        h = head_of(t)
        for i, ref in enumerate((q_ref, k_ref, v_ref)):
            block = jnp.dot(forth, ref[h], preferred_element_type=f32)
            packed[:, :, aligned(3 * t + i, depth)] = block.astype(bf16).reshape(frames, group, depth)
        return carry

    chunks = slot_chunks(slots)

    def qkv_copy(c, d, to, slot):
        first, last = chunks[c]
        lanes = pl.ds(3 * first * depth, 3 * (last - first) * depth)
        return remote(
            packed.at[to, :, lanes], moved.at[slot, :, lanes],
            qkv_send.at[c, d], qkv_recv.at[c, d], to, m,
        )

    for c, (first, last) in enumerate(chunks):
        lax.fori_loop(first, last, pack, 0)

        @each(1, frames)
        def _(d):
            qkv_copy(c, d, (me + d) % frames, me).start()

    moved[me] = packed[me]

    @pl.when(m != core)
    def _():
        w1_copy(0, p, p, m).wait_send()

    @pl.when(m == core)
    def _():
        own_copy.wait()
        for d in range(PLANE):
            source = (p + PLANE - d) % PLANE
            if d:
                w1_copy(d, p, source, m).wait_recv()
            w1_copy(d, p, source, 1 - m).wait_recv()

    for d in range(1, PLANE):
        w1_copy(d, (p + d) % PLANE, p, m).wait_send()

    def line_copy(half, b, way, to):
        ref = w_rows.at[half, pl.ds(b * PLANE * w_part, PLANE * w_part)]
        return remote(ref, ref, w2_send.at[half, b, way], w2_recv.at[half, b], to * PLANE + p, m)

    def line_round(step, half):
        for b in range(half_layers):
            distance = z - (m * half_layers + b)
            if step:
                @pl.when(jnp.logical_or(distance == step, distance == -step))
                def _():
                    line_copy(half, b, 0, z).wait_recv()

            @pl.when(jnp.logical_and(distance == step, z < layers - 1))
            def _():
                line_copy(half, b, 0, z + 1).start()

            @pl.when(jnp.logical_and(distance == -step, z > 0))
            def _():
                line_copy(half, b, 1, z - 1).start()

    def line_end(half):
        for b in range(half_layers):
            distance = z - (m * half_layers + b)

            @pl.when(jnp.logical_and(distance >= 0, z < layers - 1))
            def _():
                line_copy(half, b, 0, z).wait_send()

            @pl.when(jnp.logical_and(distance <= 0, z > 0))
            def _():
                line_copy(half, b, 1, z).wait_send()

    line_round(0, 0)
    line_round(0, 1)

    row_ids = lax.broadcasted_iota(jnp.int32, (rows, rows), 0)
    col_ids = lax.broadcasted_iota(jnp.int32, (rows, rows), 1)
    block = rows // 2
    part = block // frames
    assert 2 * block == rows and 2 * part == group

    def attend(q, k, v, t, row_block, col_block):
        levels = bias_ref[t]
        levels = jnp.concatenate([levels, levels], axis=1)
        first = col_block[0:1] == 0
        upper = jnp.where(first, levels[0:1], levels[1:2])
        lower = jnp.where(first, levels[2:3], levels[3:4])
        bias = jnp.where(row_block == 0, upper, lower)
        scores = lax.dot_general(q, k, (((1,), (1,)), ((), ())), preferred_element_type=f32)
        scores = scores * scale + bias
        weights = jnp.exp(scores - jnp.max(scores, axis=1, keepdims=True))
        total = jnp.sum(weights, axis=1, keepdims=True)
        mixed = jnp.dot(weights.astype(bf16), v, preferred_element_type=f32)
        return (mixed / total).astype(bf16)

    def attend_slots(first, last, load, blocks, store):
        def step(start, count):
            loaded = [load(start + i) for i in range(count)]
            mixed = [attend(*loaded[i], start + i, *blocks) for i in range(count)]
            for i in range(count):
                store(start + i, mixed[i])

        @each(0, (last - first) // 2)
        def _(pair):
            step(first + 2 * pair, 2)

        if (last - first) % 2:
            step(last - 1, 1)

    near_blocks = (row_ids // block, col_ids // block)
    far_blocks = ((row_ids % group) // part, (col_ids % group) // part)

    def near_load(t):
        h = head_of(t)
        return q_ref[h], k_ref[h], v_ref[h]

    def near_store(t, mixed):
        attended[p, :, aligned(t, depth)] = mixed

    def far_load(t):
        return [moved[:, :, aligned(3 * t + i, depth)].reshape(rows, depth) for i in range(3)]

    def far_store(t, mixed):
        result[:, :, aligned(t, depth)] = mixed.reshape(frames, group, depth)

    near_cols = pl.ds(slots * depth, (heads - slots) * depth)

    def near_copy(d, to, source):
        ref = attended.at[source, :, near_cols]
        return remote(ref, ref, near_send.at[d], near_recv.at[d], z * PLANE + to, m)

    def far_copy(c, d, to, source):
        first, last = chunks[c]
        ref = attended.at[source, :, pl.ds(first * depth, (last - first) * depth)]
        return remote(ref, ref, far_send.at[c, d], far_recv.at[c, d], z * PLANE + to, m)

    if slots < heads:
        attend_slots(slots, heads, near_load, near_blocks, near_store)
        for d in range(1, PLANE):
            near_copy(d, (p + d) % PLANE, p).start()

    def res_copy(c, d, to, slot):
        first, last = chunks[c]
        lanes = pl.ds(first * depth, (last - first) * depth)
        return remote(
            result.at[to, :, lanes], returned.at[slot, :, lanes],
            res_send.at[c, d], res_recv.at[c, d], to, m,
        )

    for c, (first, last) in enumerate(chunks):
        @each(1, frames)
        def _(d):
            qkv_copy(c, d, me, (me + frames - d) % frames).wait_recv()

        attend_slots(first, last, far_load, far_blocks, far_store)

        @each(1, frames)
        def _(d):
            res_copy(c, d, (me + d) % frames, me).start()

        if c < 2:
            line_round(1, c)

    returned[me] = result[me]
    line_round(2, 0)
    attend_slots(0, slots, near_load, near_blocks, near_store)

    def unpack(t, carry):
        at = aligned(t, depth)
        rows_back = jnp.dot(back, returned[:, :, at].reshape(rows, depth), preferred_element_type=f32)
        temporal = kinds_ref[:, at] == 1
        attended[p, :, at] = jnp.where(temporal, rows_back, attended[p, :, at].astype(f32)).astype(bf16)
        return carry

    for c, (first, last) in enumerate(chunks):
        @each(1, frames)
        def _(d):
            res_copy(c, d, me, (me + frames - d) % frames).wait_recv()

        lax.fori_loop(first, last, unpack, 0)
        for d in range(1, PLANE):
            far_copy(c, d, (p + d) % PLANE, p).start()
        if c == 0:
            line_round(2, 1)

    for half in range(2):
        for step in range(3, layers):
            line_round(step, half)
        line_end(half)

    @each(0, heads)
    def _(t):
        h = head_of(t)
        for half in range(2):
            for i in range(pieces):
                w_slots[half, aligned(t * pieces + i, unit), :] = w_rows[half, h * pieces + i]

    def part_copy(d):
        return remote(part_out.at[d], part_in.at[d], p_send.at[d], p_recv.at[d], me, 1 - m)

    @each(0, PLANE)
    def _(d):
        source = (p + PLANE - d) % PLANE

        @pl.when(d > 0)
        def _():
            if slots < heads:
                near_copy(d, p, source).wait_recv()
            for c in range(len(chunks)):
                far_copy(c, d, p, source).wait_recv()

        rows_in = attended[source]
        part_out[d] = jnp.dot(rows_in, w_slots[1 - m], preferred_element_type=f32)
        part_copy(d).start()
        part_own[d] = jnp.dot(rows_in, w_slots[m], preferred_element_type=f32)

    gate = gate_ref[:, aligned(p, columns)]

    def done_copy(d, to, source):
        return remote(
            done_out.at[d], done.at[:, aligned(source, columns)],
            o_send.at[d], o_recv.at[d], z * PLANE + to, m,
        )

    def gated(d):
        part_copy(d).wait_recv()
        return (gate * (part_own[d] + part_in[d])).astype(bf16)

    done[:, aligned(p, columns)] = gated(0)

    @each(1, PLANE)
    def _(d):
        done_out[d] = gated(d)
        done_copy(d, (p + PLANE - d) % PLANE, p).start()

    @each(1, frames)
    def _(d):
        for c in range(len(chunks)):
            qkv_copy(c, d, (me + d) % frames, me).wait_send()
            res_copy(c, d, (me + d) % frames, me).wait_send()

    part_copy(0).wait_send()

    @each(1, PLANE)
    def _(d):
        part_copy(d).wait_send()
        if slots < heads:
            near_copy(d, (p + d) % PLANE, p).wait_send()
        for c in range(len(chunks)):
            far_copy(c, d, (p + d) % PLANE, p).wait_send()
        done_copy(d, (p + PLANE - d) % PLANE, p).wait_send()
        done_copy(d, p, (p + d) % PLANE).wait_recv()

    out_ref[...] = done[...]


def branch_call(frames, slots, head_order, slot_kinds, slot_bias, order_map, q, k, v, w, gate):
    rows, width = q.shape
    heads = slot_bias.shape[0]
    depth = width // heads
    group, columns = rows // frames, width // PLANE
    half = w.shape[0] * frames // 2
    parts = len(slot_chunks(slots))
    unit = math.gcd(w.shape[0], depth)
    half_layers = frames // PLANE // 2
    bf16, f32, dma = jnp.bfloat16, jnp.float32, pltpu.SemaphoreType.DMA
    smem, vmem = pl.BlockSpec(memory_space=pltpu.SMEM), pl.BlockSpec(memory_space=pltpu.VMEM)
    return pl.pallas_call(
        functools.partial(branch_kernel, frames, slots, depth),
        out_shape=jax.ShapeDtypeStruct((rows, width), bf16),
        in_specs=[smem] + [pl.BlockSpec(memory_space=pl.ANY)] * 8,
        out_specs=vmem,
        scratch_shapes=[
            pltpu.VMEM(slot_kinds.shape, jnp.int32),
            pltpu.VMEM(slot_bias.shape, f32),
            pltpu.VMEM((1, rows), jnp.int32),
            pltpu.VMEM((heads, rows, depth), bf16),
            pltpu.VMEM((heads, rows, depth), bf16),
            pltpu.VMEM((heads, rows, depth), bf16),
            pltpu.VMEM((1, width), f32),
            dma((4,)),
            dma((3, heads)),
            pltpu.VMEM((frames, group, 3 * slots * depth), bf16),
            pltpu.VMEM((frames, group, 3 * slots * depth), bf16),
            pltpu.VMEM((frames, group, slots * depth), bf16),
            pltpu.VMEM((frames, group, slots * depth), bf16),
            pltpu.VMEM((PLANE, rows, width), bf16),
            pltpu.VMEM((2, half // unit, unit, columns), bf16),
            pltpu.VMEM((2, half, columns), bf16),
            pltpu.VMEM((PLANE, rows, columns), f32),
            pltpu.VMEM((PLANE, rows, columns), f32),
            pltpu.VMEM((PLANE, rows, columns), f32),
            pltpu.VMEM((PLANE, rows, columns), bf16),
            pltpu.VMEM((rows, width), bf16),
            dma((parts, frames)), dma((parts, frames)), dma((parts, frames)), dma((parts, frames)),
            dma((PLANE,)), dma((PLANE,)), dma((parts, PLANE)), dma((parts, PLANE)),
            dma((PLANE,)), dma((PLANE, 2)), dma(()), dma((2, half_layers, 2)), dma((2, half_layers)),
            dma((PLANE,)), dma((PLANE,)), dma((PLANE,)), dma((PLANE,)),
        ],
        compiler_params=pltpu.CompilerParams(
            collective_id=slots, has_side_effects=True, vmem_limit_bytes=48 * 2**20
        ),
        name="branch_%d" % slots,
    )(
        head_order, slot_kinds, slot_bias, order_map.reshape(1, rows),
        q, k, v, w.reshape(-1, unit, width), gate.reshape(1, width),
    )


def count_kernel(sizes, kinds_ref, row_ref, branch_ref, order_ref, mine, other, send, recv):
    me, m = lax.axis_index("seq"), lax.axis_index("mlp")
    heads = kinds_ref.shape[0]
    barrier = pltpu.get_barrier_semaphore()
    pl.semaphore_signal(barrier, inc=1, device_id=(me, 1 - m), device_id_type=MESH)
    mine[...] = jnp.zeros_like(mine)
    mine[0:1, 0:heads] = row_ref[...]
    pl.semaphore_wait(barrier, 1)
    copy = pltpu.make_async_remote_copy(
        src_ref=mine, dst_ref=other, send_sem=send, recv_sem=recv,
        device_id=(me, 1 - m), device_id_type=MESH,
    )
    copy.start()
    kinds = [kinds_ref[h] for h in range(heads)]
    far, near, slots = 0, sum(kinds), []
    for kind in kinds:
        slots.append(kind * far + (1 - kind) * near)
        far, near = far + kind, near + 1 - kind
    for t in range(heads):
        order_ref[t] = sum(h * (slots[h] == t).astype(jnp.int32) for h in range(heads))
    copy.wait()
    most = jnp.maximum(jnp.sum(mine[...]), jnp.sum(other[...]))
    branch_ref[0] = sum((most > size).astype(jnp.int32) for size in sizes)


def choose(sizes, head_kinds):
    heads = head_kinds.shape[0]
    smem, dma = pl.BlockSpec(memory_space=pltpu.SMEM), pltpu.SemaphoreType.DMA
    return pl.pallas_call(
        functools.partial(count_kernel, sizes),
        out_shape=[jax.ShapeDtypeStruct((1,), jnp.int32), jax.ShapeDtypeStruct((heads,), jnp.int32)],
        in_specs=[smem, pl.BlockSpec(memory_space=pltpu.VMEM)],
        out_specs=[smem, smem],
        scratch_shapes=[pltpu.VMEM((8, 128), jnp.int32)] * 2 + [dma(()), dma(())],
        compiler_params=pltpu.CompilerParams(collective_id=64, has_side_effects=True),
        name="count_temporal",
    )(head_kinds, head_kinds[None, :])


def fused_local(q, k, v, head_kinds, block_masks, order_map, out_weight, gate_values):
    frames = lax.axis_size("seq")
    heads = head_kinds.shape[0]
    depth = q.shape[1] // heads
    sizes = list(range(heads // 2 - 1, heads // 2 + 4))
    branch, order = choose(sizes, head_kinds)
    ids = jnp.arange(heads, dtype=jnp.int32)
    bias = jnp.where(block_masks == 1, 0.0, -1e30).reshape(heads, 4)
    spread = lambda kinds: jnp.repeat(kinds, depth)[None, :]
    widen = lambda levels: jnp.broadcast_to(levels[:, :, None], (heads, 4, depth))

    def by_slot(slots):
        chosen = order[:, None] == ids[None, :]
        kinds = jnp.sum(jnp.where(chosen, head_kinds[None, :], 0), axis=1)
        levels = jnp.sum(jnp.where(chosen[:, :, None], bias[None, :, :], 0.0), axis=1)
        return call(slots, order, kinds, levels)

    def call(slots, order, kinds, bias):
        return branch_call(
            frames, slots, order, spread(kinds), widen(bias),
            order_map, q, k, v, out_weight, gate_values,
        )

    branches = [functools.partial(by_slot, size) for size in sizes]
    branches.append(functools.partial(call, heads, ids, head_kinds, bias))
    return lax.switch(branch[0], branches)


def fits(mesh):
    frames = mesh.shape["seq"]
    return mesh.shape["mlp"] == 2 and frames % (2 * PLANE) == 0 and frames <= 16


def solution(mesh):
    in_specs = (
        P("seq", "mlp"),
        P("seq", "mlp"),
        P("seq", "mlp"),
        P("mlp"),
        P("mlp", None, None),
        P(),
        P("seq", "mlp"),
        P("mlp"),
    )
    out_specs = P("seq", "mlp")
    body = fused_local if fits(mesh) else local
    return jax.shard_map(body, mesh=mesh, in_specs=in_specs, out_specs=out_specs, check_vma=False)
```

```python
import functools
import math

import jax
import jax.numpy as jnp
from jax import lax
from jax.experimental import pallas as pl
from jax.experimental.pallas import tpu as pltpu
from jax.sharding import PartitionSpec as P


def attend_rows(query_rows, key_rows, value_rows, visible):
    row_count, head_count, head_depth = query_rows.shape
    score_scale = 1.0 / math.sqrt(head_depth)
    scores = (
        jnp.einsum("qhd,khd->hqk", query_rows, key_rows, preferred_element_type=jnp.float32)
        * score_scale
    )
    row_max = jnp.max(jnp.where(visible, scores, -jnp.inf), axis=2, keepdims=True)
    weights = jnp.where(visible, jnp.exp(scores - row_max), 0.0)
    row_total = jnp.sum(weights, axis=2)
    combined = jnp.einsum(
        "hqk,khd->qhd", weights.astype(jnp.bfloat16), value_rows, preferred_element_type=jnp.float32
    )
    outputs = (combined / jnp.transpose(row_total)[:, :, None]).astype(jnp.bfloat16)
    return outputs


def to_positions(query_rows, key_rows, value_rows, frames, group_size):
    row_width = query_rows.shape[1]
    exchanged = (
        lax.all_to_all(
            query_rows.reshape(frames, group_size, 1, row_width),
            "seq",
            split_axis=0,
            concat_axis=2,
            tiled=True,
        ),
        lax.all_to_all(
            key_rows.reshape(frames, group_size, 1, row_width),
            "seq",
            split_axis=0,
            concat_axis=2,
            tiled=True,
        ),
        lax.all_to_all(
            value_rows.reshape(frames, group_size, 1, row_width),
            "seq",
            split_axis=0,
            concat_axis=2,
            tiled=True,
        ),
    )
    return tuple((member.reshape(group_size * frames, row_width) for member in exchanged))


def to_frames(results, frames, group_size):
    row_width = results.shape[1]
    exchanged = lax.all_to_all(
        results.reshape(1, group_size, frames, row_width),
        "seq",
        split_axis=2,
        concat_axis=0,
        tiled=True,
    )
    return exchanged.reshape(frames * group_size, row_width)


def split_heads(array, head_count):
    return array.reshape(array.shape[0], head_count, array.shape[1] // head_count)


def local(
    queries, key_vectors, value_vectors, head_kinds, block_masks, order_map, out_weight, gate_values
):
    row_count, row_width = queries.shape
    head_count = head_kinds.shape[0]
    frames = lax.axis_size("seq")
    group_size = row_count // frames
    block_size = row_count // block_masks.shape[1]
    inverse = (
        jnp.zeros((row_count,), jnp.int32).at[order_map].set(jnp.arange(row_count, dtype=jnp.int32))
    )
    visible = jnp.repeat(jnp.repeat(block_masks == 1, block_size, axis=1), block_size, axis=2)
    temporal = (head_kinds == 1)[None, :, None]
    moved_queries, moved_keys, moved_values = to_positions(
        queries[order_map], key_vectors[order_map], value_vectors[order_map], frames, group_size
    )
    near_result = attend_rows(
        split_heads(queries, head_count),
        split_heads(key_vectors, head_count),
        split_heads(value_vectors, head_count),
        visible,
    )
    far_result = attend_rows(
        split_heads(moved_queries, head_count),
        split_heads(moved_keys, head_count),
        split_heads(moved_values, head_count),
        visible,
    )
    returned = to_frames(far_result.reshape(row_count, row_width), frames, group_size)[inverse]
    per_head = jnp.where(temporal, split_heads(returned, head_count), near_result)
    attended = per_head.reshape(row_count, row_width)
    head_columns = lax.all_gather(attended, "mlp", axis=1, tiled=True)
    projected = jnp.dot(
        head_columns,
        lax.all_gather(out_weight, "seq", axis=0, tiled=True),
        preferred_element_type=jnp.float32,
    )
    return (gate_values[None, :] * projected).astype(jnp.bfloat16)


PLANE = 4
MESH = pl.DeviceIdType.MESH


def aligned(index, size):
    return pl.ds(pl.multiple_of(index * size, size), size)


def each(first, last):
    def run(body):
        def step(i, carry):
            body(i)
            return carry

        lax.fori_loop(first, last, step, 0)

    return run


def slot_chunks(slots):
    parts = max(1, min(4, slots // 2))
    edges = [-(-slots * i // parts) for i in range(parts + 1)]
    return list(zip(edges[:-1], edges[1:]))


def branch_kernel(
    frames, slots, depth,
    heads_ref, kinds_hbm, bias_hbm, order_hbm, q_hbm, k_hbm, v_hbm, w_ref, gate_hbm,
    out_ref,
    kinds_ref, bias_ref, order_ref, q_ref, k_ref, v_ref, gate_ref, fetch_sem, head_sem,
    packed, moved, result, returned, attended, w_rows, w_slots, part_out, part_in,
    done_out, done,
    qkv_send, qkv_recv, res_send, res_recv, near_send, near_recv, far_send, far_recv,
    w1_send, w1_recv, w1_own, w2_send, w2_recv, p_send, p_recv, o_send, o_recv,
):
    rows, width = q_hbm.shape
    heads = width // depth
    group = rows // frames
    layers = frames // PLANE
    half_layers = layers // 2
    w_part, unit = w_ref.shape[:2]
    pieces, columns = depth // unit, width // PLANE
    me, m = lax.axis_index("seq"), lax.axis_index("mlp")
    z, p = me // PLANE, me % PLANE
    scale = 1.0 / math.sqrt(depth)
    bf16, f32 = jnp.bfloat16, jnp.float32

    def remote(src, dst, send, recv, seq, mlp):
        return pltpu.make_async_remote_copy(
            src_ref=src, dst_ref=dst, send_sem=send, recv_sem=recv,
            device_id=(seq, mlp), device_id_type=MESH,
        )

    fetches = [
        pltpu.make_async_copy(src, dst, fetch_sem.at[i])
        for i, (src, dst) in enumerate((
            (order_hbm, order_ref), (bias_hbm, bias_ref), (kinds_hbm, kinds_ref), (gate_hbm, gate_ref),
        ))
    ]

    def head_fetches(h):
        return [
            pltpu.make_async_copy(src.at[:, aligned(h, depth)], dst.at[h], head_sem.at[i, h])
            for i, (src, dst) in enumerate(((q_hbm, q_ref), (k_hbm, k_ref), (v_hbm, v_ref)))
        ]

    for fetch in fetches:
        fetch.start()

    @each(0, heads)
    def _(h):
        for fetch in head_fetches(h):
            fetch.start()

    barrier = pltpu.get_barrier_semaphore()
    pl.semaphore_signal(barrier, inc=1, device_id=(me, 1 - m), device_id_type=MESH)

    @each(1, frames)
    def _(d):
        peer = (me + d) % frames
        pl.semaphore_signal(barrier, inc=1, device_id=(peer, m), device_id_type=MESH)
        pl.semaphore_signal(barrier, inc=1, device_id=(peer, 1 - m), device_id_type=MESH)

    pl.semaphore_wait(barrier, 2 * frames - 1)

    core = z // half_layers
    layer = z % half_layers

    def w1_copy(d, to, source, source_m):
        return remote(
            w_ref.at[:, :, aligned(to, columns)],
            w_rows.at[source_m, aligned(layer * PLANE + source, w_part)],
            w1_send.at[d], w1_recv.at[d, source_m], z * PLANE + to, core,
        )

    for d in range(1, PLANE):
        w1_copy(d, (p + d) % PLANE, p, m).start()

    @pl.when(m != core)
    def _():
        w1_copy(0, p, p, m).start()

    own_copy = pltpu.make_async_copy(
        w_ref.at[:, :, aligned(p, columns)],
        w_rows.at[m, aligned(layer * PLANE + p, w_part)],
        w1_own,
    )

    @pl.when(m == core)
    def _():
        own_copy.start()

    for fetch in fetches:
        fetch.wait()

    @each(0, heads)
    def _(h):
        for fetch in head_fetches(h):
            fetch.wait()

    places = lax.broadcasted_iota(jnp.int32, (rows, rows), 0)
    back_f32 = jnp.where(places == order_ref[...], 1.0, 0.0)
    back = back_f32.astype(bf16)
    forth = back_f32.T.astype(bf16)

    def head_of(t):
        return t if slots == heads else heads_ref[t]

    def pack(t, carry):
        h = head_of(t)
        for i, ref in enumerate((q_ref, k_ref, v_ref)):
            block = jnp.dot(forth, ref[h], preferred_element_type=f32)
            packed[:, :, aligned(3 * t + i, depth)] = block.astype(bf16).reshape(frames, group, depth)
        return carry

    chunks = slot_chunks(slots)

    def qkv_copy(c, d, to, slot):
        first, last = chunks[c]
        lanes = pl.ds(3 * first * depth, 3 * (last - first) * depth)
        return remote(
            packed.at[to, :, lanes], moved.at[slot, :, lanes],
            qkv_send.at[c, d], qkv_recv.at[c, d], to, m,
        )

    for c, (first, last) in enumerate(chunks):
        lax.fori_loop(first, last, pack, 0)

        @each(1, frames)
        def _(d):
            qkv_copy(c, d, (me + d) % frames, me).start()

    moved[me] = packed[me]

    @pl.when(m != core)
    def _():
        w1_copy(0, p, p, m).wait_send()

    @pl.when(m == core)
    def _():
        own_copy.wait()
        for d in range(PLANE):
            source = (p + PLANE - d) % PLANE
            if d:
                w1_copy(d, p, source, m).wait_recv()
            w1_copy(d, p, source, 1 - m).wait_recv()

    for d in range(1, PLANE):
        w1_copy(d, (p + d) % PLANE, p, m).wait_send()

    def line_copy(half, b, way, to):
        ref = w_rows.at[half, pl.ds(b * PLANE * w_part, PLANE * w_part)]
        return remote(ref, ref, w2_send.at[half, b, way], w2_recv.at[half, b], to * PLANE + p, m)

    def line_round(step, half):
        for b in range(half_layers):
            distance = z - (m * half_layers + b)
            if step:
                @pl.when(jnp.logical_or(distance == step, distance == -step))
                def _():
                    line_copy(half, b, 0, z).wait_recv()

            @pl.when(jnp.logical_and(distance == step, z < layers - 1))
            def _():
                line_copy(half, b, 0, z + 1).start()

            @pl.when(jnp.logical_and(distance == -step, z > 0))
            def _():
                line_copy(half, b, 1, z - 1).start()

    def line_end(half):
        for b in range(half_layers):
            distance = z - (m * half_layers + b)

            @pl.when(jnp.logical_and(distance >= 0, z < layers - 1))
            def _():
                line_copy(half, b, 0, z).wait_send()

            @pl.when(jnp.logical_and(distance <= 0, z > 0))
            def _():
                line_copy(half, b, 1, z).wait_send()

    line_round(0, 0)
    line_round(0, 1)

    row_ids = lax.broadcasted_iota(jnp.int32, (rows, rows), 0)
    col_ids = lax.broadcasted_iota(jnp.int32, (rows, rows), 1)
    block = rows // 2
    part = block // frames
    assert 2 * block == rows and 2 * part == group

    def attend(q, k, v, t, row_block, col_block):
        levels = bias_ref[t]
        levels = jnp.concatenate([levels, levels], axis=1)
        first = col_block[0:1] == 0
        upper = jnp.where(first, levels[0:1], levels[1:2])
        lower = jnp.where(first, levels[2:3], levels[3:4])
        bias = jnp.where(row_block == 0, upper, lower)
        scores = lax.dot_general(q, k, (((1,), (1,)), ((), ())), preferred_element_type=f32)
        scores = scores * scale + bias
        weights = jnp.exp(scores - jnp.max(scores, axis=1, keepdims=True))
        total = jnp.sum(weights, axis=1, keepdims=True)
        mixed = jnp.dot(weights.astype(bf16), v, preferred_element_type=f32)
        return (mixed / total).astype(bf16)

    def attend_slots(first, last, load, blocks, store):
        def step(start, count):
            loaded = [load(start + i) for i in range(count)]
            mixed = [attend(*loaded[i], start + i, *blocks) for i in range(count)]
            for i in range(count):
                store(start + i, mixed[i])

        @each(0, (last - first) // 2)
        def _(pair):
            step(first + 2 * pair, 2)

        if (last - first) % 2:
            step(last - 1, 1)

    near_blocks = (row_ids // block, col_ids // block)
    far_blocks = ((row_ids % group) // part, (col_ids % group) // part)

    def near_load(t):
        h = head_of(t)
        return q_ref[h], k_ref[h], v_ref[h]

    def near_store(t, mixed):
        attended[p, :, aligned(t, depth)] = mixed

    def far_load(t):
        return [moved[:, :, aligned(3 * t + i, depth)].reshape(rows, depth) for i in range(3)]

    def far_store(t, mixed):
        result[:, :, aligned(t, depth)] = mixed.reshape(frames, group, depth)

    near_cols = pl.ds(slots * depth, (heads - slots) * depth)

    def near_copy(d, to, source):
        ref = attended.at[source, :, near_cols]
        return remote(ref, ref, near_send.at[d], near_recv.at[d], z * PLANE + to, m)

    def far_copy(c, d, to, source):
        first, last = chunks[c]
        ref = attended.at[source, :, pl.ds(first * depth, (last - first) * depth)]
        return remote(ref, ref, far_send.at[c, d], far_recv.at[c, d], z * PLANE + to, m)

    if slots < heads:
        attend_slots(slots, heads, near_load, near_blocks, near_store)
        for d in range(1, PLANE):
            near_copy(d, (p + d) % PLANE, p).start()

    def res_copy(c, d, to, slot):
        first, last = chunks[c]
        lanes = pl.ds(first * depth, (last - first) * depth)
        return remote(
            result.at[to, :, lanes], returned.at[slot, :, lanes],
            res_send.at[c, d], res_recv.at[c, d], to, m,
        )

    for c, (first, last) in enumerate(chunks):
        @each(1, frames)
        def _(d):
            qkv_copy(c, d, me, (me + frames - d) % frames).wait_recv()

        attend_slots(first, last, far_load, far_blocks, far_store)

        @each(1, frames)
        def _(d):
            res_copy(c, d, (me + d) % frames, me).start()

        if c < 2:
            line_round(1, c)

    returned[me] = result[me]
    line_round(2, 0)
    attend_slots(0, slots, near_load, near_blocks, near_store)
    line_round(2, 1)

    def unpack(t, carry):
        at = aligned(t, depth)
        rows_back = jnp.dot(back, returned[:, :, at].reshape(rows, depth), preferred_element_type=f32)
        temporal = kinds_ref[:, at] == 1
        attended[p, :, at] = jnp.where(temporal, rows_back, attended[p, :, at].astype(f32)).astype(bf16)
        return carry

    for c, (first, last) in enumerate(chunks):
        @each(1, frames)
        def _(d):
            res_copy(c, d, me, (me + frames - d) % frames).wait_recv()

        lax.fori_loop(first, last, unpack, 0)
        for d in range(1, PLANE):
            far_copy(c, d, (p + d) % PLANE, p).start()
    for half in range(2):
        for step in range(3, layers):
            line_round(step, half)
        line_end(half)

    @each(0, heads)
    def _(t):
        h = head_of(t)
        for half in range(2):
            for i in range(pieces):
                w_slots[half, aligned(t * pieces + i, unit), :] = w_rows[half, h * pieces + i]

    def part_copy(d):
        return remote(part_out.at[d], part_in.at[d], p_send.at[d], p_recv.at[d], me, 1 - m)

    @each(0, PLANE)
    def _(d):
        source = (p + PLANE - d) % PLANE

        @pl.when(d > 0)
        def _():
            if slots < heads:
                near_copy(d, p, source).wait_recv()
            for c in range(len(chunks)):
                far_copy(c, d, p, source).wait_recv()

        part_out[d] = jnp.dot(attended[source], w_slots[1 - m], preferred_element_type=f32)
        part_copy(d).start()

    gate = gate_ref[:, aligned(p, columns)]

    def done_copy(d, to, source):
        return remote(
            done_out.at[d], done.at[:, aligned(source, columns)],
            o_send.at[d], o_recv.at[d], z * PLANE + to, m,
        )

    def gated(d):
        rows_in = attended[(p + PLANE - d) % PLANE]
        part_own = jnp.dot(rows_in, w_slots[m], preferred_element_type=f32)
        part_copy(d).wait_recv()
        return (gate * (part_own + part_in[d])).astype(bf16)

    @each(1, PLANE)
    def _(d):
        done_out[d] = gated(d)
        done_copy(d, (p + PLANE - d) % PLANE, p).start()

    done[:, aligned(p, columns)] = gated(0)

    @each(1, frames)
    def _(d):
        for c in range(len(chunks)):
            qkv_copy(c, d, (me + d) % frames, me).wait_send()
            res_copy(c, d, (me + d) % frames, me).wait_send()

    part_copy(0).wait_send()

    @each(1, PLANE)
    def _(d):
        part_copy(d).wait_send()
        if slots < heads:
            near_copy(d, (p + d) % PLANE, p).wait_send()
        for c in range(len(chunks)):
            far_copy(c, d, (p + d) % PLANE, p).wait_send()
        done_copy(d, (p + PLANE - d) % PLANE, p).wait_send()
        done_copy(d, p, (p + d) % PLANE).wait_recv()

    out_ref[...] = done[...]


def branch_call(frames, slots, head_order, slot_kinds, slot_bias, order_map, q, k, v, w, gate):
    rows, width = q.shape
    heads = slot_bias.shape[0]
    depth = width // heads
    group, columns = rows // frames, width // PLANE
    half = w.shape[0] * frames // 2
    parts = len(slot_chunks(slots))
    unit = math.gcd(w.shape[0], depth)
    half_layers = frames // PLANE // 2
    bf16, f32, dma = jnp.bfloat16, jnp.float32, pltpu.SemaphoreType.DMA
    smem, vmem = pl.BlockSpec(memory_space=pltpu.SMEM), pl.BlockSpec(memory_space=pltpu.VMEM)
    return pl.pallas_call(
        functools.partial(branch_kernel, frames, slots, depth),
        out_shape=jax.ShapeDtypeStruct((rows, width), bf16),
        in_specs=[smem] + [pl.BlockSpec(memory_space=pl.ANY)] * 8,
        out_specs=vmem,
        scratch_shapes=[
            pltpu.VMEM(slot_kinds.shape, jnp.int32),
            pltpu.VMEM(slot_bias.shape, f32),
            pltpu.VMEM((1, rows), jnp.int32),
            pltpu.VMEM((heads, rows, depth), bf16),
            pltpu.VMEM((heads, rows, depth), bf16),
            pltpu.VMEM((heads, rows, depth), bf16),
            pltpu.VMEM((1, width), f32),
            dma((4,)),
            dma((3, heads)),
            pltpu.VMEM((frames, group, 3 * slots * depth), bf16),
            pltpu.VMEM((frames, group, 3 * slots * depth), bf16),
            pltpu.VMEM((frames, group, slots * depth), bf16),
            pltpu.VMEM((frames, group, slots * depth), bf16),
            pltpu.VMEM((PLANE, rows, width), bf16),
            pltpu.VMEM((2, half // unit, unit, columns), bf16),
            pltpu.VMEM((2, half, columns), bf16),
            pltpu.VMEM((PLANE, rows, columns), f32),
            pltpu.VMEM((PLANE, rows, columns), f32),
            pltpu.VMEM((PLANE, rows, columns), bf16),
            pltpu.VMEM((rows, width), bf16),
            dma((parts, frames)), dma((parts, frames)), dma((parts, frames)), dma((parts, frames)),
            dma((PLANE,)), dma((PLANE,)), dma((parts, PLANE)), dma((parts, PLANE)),
            dma((PLANE,)), dma((PLANE, 2)), dma(()), dma((2, half_layers, 2)), dma((2, half_layers)),
            dma((PLANE,)), dma((PLANE,)), dma((PLANE,)), dma((PLANE,)),
        ],
        compiler_params=pltpu.CompilerParams(
            collective_id=slots, has_side_effects=True, vmem_limit_bytes=48 * 2**20
        ),
        name="branch_%d" % slots,
    )(
        head_order, slot_kinds, slot_bias, order_map.reshape(1, rows),
        q, k, v, w.reshape(-1, unit, width), gate.reshape(1, width),
    )


def count_kernel(sizes, kinds_ref, row_ref, branch_ref, order_ref, mine, other, send, recv):
    me, m = lax.axis_index("seq"), lax.axis_index("mlp")
    heads = kinds_ref.shape[0]
    barrier = pltpu.get_barrier_semaphore()
    pl.semaphore_signal(barrier, inc=1, device_id=(me, 1 - m), device_id_type=MESH)
    mine[...] = jnp.zeros_like(mine)
    mine[0:1, 0:heads] = row_ref[...]
    pl.semaphore_wait(barrier, 1)
    copy = pltpu.make_async_remote_copy(
        src_ref=mine, dst_ref=other, send_sem=send, recv_sem=recv,
        device_id=(me, 1 - m), device_id_type=MESH,
    )
    copy.start()
    kinds = [kinds_ref[h] for h in range(heads)]
    far, near, slots = 0, sum(kinds), []
    for kind in kinds:
        slots.append(kind * far + (1 - kind) * near)
        far, near = far + kind, near + 1 - kind
    for t in range(heads):
        order_ref[t] = sum(h * (slots[h] == t).astype(jnp.int32) for h in range(heads))
    copy.wait()
    most = jnp.maximum(jnp.sum(mine[...]), jnp.sum(other[...]))
    branch_ref[0] = sum((most > size).astype(jnp.int32) for size in sizes)


def choose(sizes, head_kinds):
    heads = head_kinds.shape[0]
    smem, dma = pl.BlockSpec(memory_space=pltpu.SMEM), pltpu.SemaphoreType.DMA
    return pl.pallas_call(
        functools.partial(count_kernel, sizes),
        out_shape=[jax.ShapeDtypeStruct((1,), jnp.int32), jax.ShapeDtypeStruct((heads,), jnp.int32)],
        in_specs=[smem, pl.BlockSpec(memory_space=pltpu.VMEM)],
        out_specs=[smem, smem],
        scratch_shapes=[pltpu.VMEM((8, 128), jnp.int32)] * 2 + [dma(()), dma(())],
        compiler_params=pltpu.CompilerParams(collective_id=64, has_side_effects=True),
        name="count_temporal",
    )(head_kinds, head_kinds[None, :])


def fused_local(q, k, v, head_kinds, block_masks, order_map, out_weight, gate_values):
    frames = lax.axis_size("seq")
    heads = head_kinds.shape[0]
    depth = q.shape[1] // heads
    sizes = list(range(heads // 2 - 1, heads // 2 + 4))
    branch, order = choose(sizes, head_kinds)
    ids = jnp.arange(heads, dtype=jnp.int32)
    bias = jnp.where(block_masks == 1, 0.0, -1e30).reshape(heads, 4)
    spread = lambda kinds: jnp.repeat(kinds, depth)[None, :]
    widen = lambda levels: jnp.broadcast_to(levels[:, :, None], (heads, 4, depth))

    def by_slot(slots):
        chosen = order[:, None] == ids[None, :]
        kinds = jnp.sum(jnp.where(chosen, head_kinds[None, :], 0), axis=1)
        levels = jnp.sum(jnp.where(chosen[:, :, None], bias[None, :, :], 0.0), axis=1)
        return call(slots, order, kinds, levels)

    def call(slots, order, kinds, bias):
        return branch_call(
            frames, slots, order, spread(kinds), widen(bias),
            order_map, q, k, v, out_weight, gate_values,
        )

    branches = [functools.partial(by_slot, size) for size in sizes]
    branches.append(functools.partial(call, heads, ids, head_kinds, bias))
    return lax.switch(branch[0], branches)


def fits(mesh):
    frames = mesh.shape["seq"]
    return mesh.shape["mlp"] == 2 and frames % (2 * PLANE) == 0 and frames <= 16


def solution(mesh):
    in_specs = (
        P("seq", "mlp"),
        P("seq", "mlp"),
        P("seq", "mlp"),
        P("mlp"),
        P("mlp", None, None),
        P(),
        P("seq", "mlp"),
        P("mlp"),
    )
    out_specs = P("seq", "mlp")
    body = fused_local if fits(mesh) else local
    return jax.shard_map(body, mesh=mesh, in_specs=in_specs, out_specs=out_specs, check_vma=False)
```
